32 devices in a mesh: grp: 2 (over x), blk: 8 (over z, y), ins: 2 (over core).
Axes of the slice: x: 2, y: 2, z: 4, core: 2. Of those that a mesh axis runs over, the one named last changes fastest.
Arguments:
- start_state: float32 [8, 6, 256, 1024], P('ins', None, 'grp', 'blk'), parts along dimension 2, may hold values from -4 to 4
- source_term: float32 [8, 6, 256, 1024], P('ins', None, 'grp', 'blk'), parts along dimension 2, may hold values from -6 to 6
- time_step: float32 [256, 1024], P('grp', 'blk'), parts along dimension 0, may hold values from 0.05 to 0.2
- wall_factor: float32 [256, 1024], P('grp', 'blk'), parts along dimension 0, may hold values from 0.1 to 1
- flux_split: float32 [2, 2, 6, 6], replicated, may hold values from -1.5 to 1.5
- stator_donor: int32 [8, 1024], P('ins', 'blk'), may hold values from 0 to 1023, as said below
- rotor_donor: int32 [8, 1024], P('ins', 'blk'), may hold values from 0 to 1023, as said below
Outputs:
- new_state: float32 [8, 6, 256, 1024], P('ins', None, 'grp', 'blk'), parts along dimension 2
The draws below stay inside these ranges and needn't reach their ends.
There are 2 independent parts, one for each index of `grp`. The reference program is written for one: setup_inputs(seed, part) draws one part's arguments, and reference() takes and returns one part's arrays. A program takes and returns all parts, laid end to end along the dimension named above; an argument that names none is the same for every part. Nothing has to cross between parts.
Inputs may be any that keep to these rules, and one draw needn't show every extreme that they name: For each instance n, stator_donor[n, j] = (j - s_n) mod 1024 for a shift s_n of that instance. For each instance n, rotor_donor[n, j] = (j + s_n) mod 1024 with the same shift s_n as stator_donor.
All inputs are finite; a program needn't handle non-finite values.
Results may differ from the reference program's by a relative error of at most 0.0001.
Values sent between devices are 32-bit elements; how exact they have to be, the bound alone decides.
A program may use at most 128 MiB of HBM per device.

```python
import math
import jax
import jax.numpy as jnp
from jax import lax

NINST = 8
NV = 6
CI = 128
NJ = 1024


def donor_shifts(key):
    return jax.random.randint(key, (NINST,), 0, NJ, dtype=jnp.int32)


def draw_stator_donor(key, part):
    shifts = donor_shifts(key)
    columns = jnp.arange(NJ, dtype=jnp.int32)
    return (columns[None, :] - shifts[:, None]) % NJ


def draw_rotor_donor(key, part):
    shifts = donor_shifts(key)
    columns = jnp.arange(NJ, dtype=jnp.int32)
    return (columns[None, :] + shifts[:, None]) % NJ


def draw_flux_split(key, part):
    key = jax.random.fold_in(key, 7)
    first_key, second_key = jax.random.split(key)
    diagonal = jnp.exp(jax.random.uniform(first_key, (2, 2, NV), jnp.float32, math.log(0.3), 0.0))
    coupling = 0.12 * jnp.clip(jax.random.normal(second_key, (2, 2, NV, NV), jnp.float32), -4.0, 4.0)
    signs = jnp.array([1.0, -1.0], dtype=jnp.float32)[None, :, None]
    identity_matrix = jnp.eye(NV, dtype=jnp.float32)
    return (signs * diagonal)[..., None] * identity_matrix + coupling


def block_levels(own_key, dims, pieces, smallest, top_value):
    factor_of = 1.0
    for position, parts in pieces:
        heights = jax.random.uniform(jax.random.fold_in(jax.random.fold_in(own_key, 6), position), (parts,), jnp.float32, smallest / len(pieces), top_value / len(pieces))
        factor_of = factor_of * jnp.repeat(jnp.exp(heights), dims[position] // parts).reshape((-1,) + (1,) * (len(dims) - 1 - position))
    return factor_of


def centred(stream_key, dims, scale, bound, pieces=(), kind=jnp.bfloat16):
    drawn = scale * jax.random.normal(stream_key, dims, jnp.float32)
    if pieces:
        drawn = drawn * block_levels(stream_key, dims, pieces, -0.22, 0.18)
    return jnp.clip(drawn, -bound, bound).astype(kind)


def setup_inputs(seed: int = 0, part: int = 0) -> dict:
    arg_keys = jax.random.split(jax.random.key(seed), 8)
    part_keys = jax.random.split(jax.random.fold_in(arg_keys[7], part), 8)
    return {
        "start_state": centred(part_keys[0], (NINST, NV, CI, NJ), 1.0, 4.0, ((0, 2), (3, 8)), jnp.float32),
        "source_term": centred(part_keys[1], (NINST, NV, CI, NJ), 1.0, 6.0, ((0, 2), (3, 8)), jnp.float32),
        "time_step": jnp.clip(jnp.exp(math.log(0.2) - 1.3862944 * jax.random.uniform(part_keys[2], (CI, NJ), jnp.float32) ** block_levels(part_keys[2], (CI, NJ), ((1, 8),), -0.2, 0.2)), 0.05, 0.2),
        "wall_factor": jnp.clip(jnp.exp(math.log(1.0) - 2.3025851 * jax.random.uniform(part_keys[3], (CI, NJ), jnp.float32) ** block_levels(part_keys[3], (CI, NJ), ((1, 8),), -0.2, 0.2)), 0.1, 1.0),
        "flux_split": draw_flux_split(jax.random.fold_in(arg_keys[7], 71), part),
        "stator_donor": draw_stator_donor(jax.random.fold_in(arg_keys[7], 71), part),
        "rotor_donor": draw_rotor_donor(jax.random.fold_in(arg_keys[7], 71), part),
    }


OMEGA = 1.0
DESTRUCTION = 2.0
SEGMENT_FACTORS = (1.0 / 3.0, 0.5, 1.0)
HIGHEST_PRECISION = lax.Precision.HIGHEST


def spectral_matrix(instances):
    levels = jnp.arange(instances, dtype=jnp.int32)
    offsets = levels[:, None] - levels[None, :]
    angles = jnp.pi * offsets.astype(jnp.float32) / instances
    parity = (1 - 2 * (jnp.abs(offsets) % 2)).astype(jnp.float32)
    denominator = jnp.where(offsets == 0, jnp.float32(1.0), jnp.sin(angles))
    values = 0.5 * OMEGA * parity * jnp.cos(angles) / denominator
    return jnp.where(offsets == 0, jnp.float32(0.0), values)


def apply_matrix(matrix, values):
    return jnp.einsum('vw,nwij->nvij', matrix, values, precision=HIGHEST_PRECISION)


def apply_row(matrix, values):
    return jnp.einsum('vw,nwj->nvj', matrix, values, precision=HIGHEST_PRECISION)


def pick_donors(donor_row, donor_list):
    gather_index = jnp.broadcast_to(donor_list[:, None, :], (donor_row.shape[0], donor_row.shape[1], donor_list.shape[1]))
    return jnp.take_along_axis(donor_row, gather_index, axis=2)


def residual_of(current, source_term, wall_factor, flux_split, stator_donor, rotor_donor, spectral):
    split_rows = current.shape[2] // 2
    plus_axial = apply_matrix(flux_split[0, 0], current)
    minus_axial = apply_matrix(flux_split[0, 1], current)
    zero_row = jnp.zeros_like(current[:, :, :1])
    right_axial = plus_axial + jnp.concatenate([minus_axial[:, :, 1:], zero_row], axis=2)
    left_axial = jnp.concatenate([zero_row, plus_axial[:, :, :-1]], axis=2) + minus_axial
    facing_rotor = pick_donors(current[:, :, split_rows], stator_donor)
    facing_stator = pick_donors(current[:, :, split_rows - 1], rotor_donor)
    right_axial = right_axial.at[:, :, split_rows - 1].set(plus_axial[:, :, split_rows - 1] + apply_row(flux_split[0, 1], facing_rotor))
    left_axial = left_axial.at[:, :, split_rows].set(apply_row(flux_split[0, 0], facing_stator) + minus_axial[:, :, split_rows])
    plus_around = apply_matrix(flux_split[1, 0], current)
    minus_around = apply_matrix(flux_split[1, 1], current)
    right_around = plus_around + jnp.roll(minus_around, -1, axis=3)
    left_around = jnp.roll(plus_around, 1, axis=3) + minus_around
    spectral_term = jnp.einsum('nm,mvij->nvij', spectral, current, precision=HIGHEST_PRECISION)
    summed = right_axial - left_axial + right_around - left_around + spectral_term - source_term
    turbulent = current[:, 5]
    return summed.at[:, 5].add(DESTRUCTION * turbulent * jnp.abs(turbulent) * wall_factor)


def reference(start_state, source_term, time_step, wall_factor, flux_split, stator_donor, rotor_donor):
    spectral = spectral_matrix(NINST)
    current = start_state
    for factor in SEGMENT_FACTORS:
        current = start_state - factor * time_step * residual_of(current, source_term, wall_factor, flux_split, stator_donor, rotor_donor, spectral)
    return current
```

```python
import functools
import math

import jax
import jax.numpy as jnp
from jax import lax
from jax.experimental import pallas as pl
from jax.experimental.pallas import tpu as pltpu
from jax.sharding import PartitionSpec as P

NINST = 8
NV = 6
CHANNELS = NINST * NV
LANES = 128
PITCH_PAD = 8
SEGMENT_FACTORS = (1.0 / 3.0, 0.5, 1.0)
MESH = pl.DeviceIdType.MESH
F32 = jnp.float32
BF16 = jnp.bfloat16


def split_stack(values):
    high = values.astype(BF16)
    low = (values - high.astype(F32)).astype(BF16)
    return jnp.concatenate([high, low, high], axis=0)


def build_weights(flux_ref, weight_ref):
    shape = (NINST, 3 * CHANNELS)
    lane = lax.broadcasted_iota(jnp.int32, shape, 1)
    instance = lax.broadcasted_iota(jnp.int32, shape, 0)
    column = (
        lane
        - jnp.where(lane >= CHANNELS, CHANNELS, 0)
        - jnp.where(lane >= 2 * CHANNELS, CHANNELS, 0)
    )
    in_component = column >> 3
    offset = instance - (column & 7)
    spectral = jnp.zeros(shape, F32)
    for d in range(1, NINST):
        value = 0.5 * (-1.0) ** d * math.cos(math.pi * d / NINST) / math.sin(math.pi * d / NINST)
        spectral = jnp.where(offset == d, F32(value), spectral)
        spectral = jnp.where(offset == -d, F32(-value), spectral)
    same = offset == 0

    def flux_row(direction, part, v):
        row = jnp.zeros(shape, F32)
        for w in range(NV):
            row = jnp.where(in_component == w, flux_ref[direction, part, v, w], row)
        return row

    rows = [[], [], [], [], []]
    for v in range(NV):
        pa, ma = flux_row(0, 0, v), flux_row(0, 1, v)
        pc, mc = flux_row(1, 0, v), flux_row(1, 1, v)
        centre = jnp.where(same, pa - ma + pc - mc, 0.0) + jnp.where(
            in_component == v, spectral, 0.0
        )
        rows[0].append(centre)
        for place, matrix in ((1, ma), (2, -pa), (3, mc), (4, -pc)):
            rows[place].append(jnp.where(same, matrix, 0.0))
    flat = [row for group in rows for row in group]
    for k in range(0, len(flat), 2):
        value = jnp.concatenate([flat[k], flat[k + 1]], axis=0)
        high = value.astype(BF16).astype(F32)
        wide = lax.broadcasted_iota(jnp.int32, value.shape, 1)
        weight_ref[k * 8 : k * 8 + 16, :] = jnp.where(
            wide < 2 * CHANNELS, high, value - high
        ).astype(BF16)


def kernel(
    blocks,
    half,
    start_hbm,
    source_hbm,
    dt_ref,
    wall_ref,
    flux_ref,
    stator_ref,
    rotor_ref,
    out_hbm,
    state0,
    state1,
    state2,
    source,
    weight_ref,
    donors,
    donor_send,
    row_send,
    row_recv,
    edge_send,
    edge_recv,
    local_sem,
    remote_send_sem,
    remote_recv_sem,
    donor_sem,
    row_send_sem,
    row_recv_sem,
    edge_send_sem,
    edge_recv_sem,
):
    me = lax.axis_index("ins")
    blk = lax.axis_index("blk")
    other = 1 - me
    per_core = start_hbm.shape[0]
    pitch = half + PITCH_PAD
    right = lax.rem(blk + 1, blocks)
    left = lax.rem(blk + blocks - 1, blocks)
    my_rows = pl.ds(pl.multiple_of(me * half, 8), half)
    other_rows = pl.ds(pl.multiple_of(other * half, 8), half)

    def local_in(array, place, buffer, n):
        return pltpu.make_async_copy(
            array.at[n, :, my_rows, :],
            buffer.at[:, per_core * me + n, pl.ds(0, half), :],
            local_sem.at[place, n],
        )

    def remote_in(array, place, buffer, n):
        return pltpu.make_async_remote_copy(
            src_ref=array.at[n, :, other_rows, :],
            dst_ref=buffer.at[:, per_core * me + n, pl.ds(0, half), :],
            send_sem=remote_send_sem.at[place, n],
            recv_sem=remote_recv_sem.at[place, n],
            device_id={"ins": other},
            device_id_type=MESH,
        )

    for n in range(per_core):
        local_in(start_hbm, 0, state0, n).start()

    barrier = pltpu.get_barrier_semaphore()
    for b in range(blocks):
        pl.semaphore_signal(barrier, inc=1, device_id={"blk": b, "ins": other}, device_id_type=MESH)
    for b in (left, right):
        pl.semaphore_signal(barrier, inc=1, device_id={"blk": b}, device_id_type=MESH)
    for n in range(per_core):
        local_in(source_hbm, 1, source, n).start()
    build_weights(flux_ref, weight_ref)
    stator = stator_ref[...]
    rotor = rotor_ref[...]
    donors[me] = jnp.where(me == 0, stator, rotor)
    donor_send[...] = jnp.where(me == 0, rotor, stator)
    pl.semaphore_wait(barrier, blocks + 2)

    for n in range(per_core):
        remote_in(start_hbm, 0, state0, n).start()
    donor_copy = pltpu.make_async_remote_copy(
        src_ref=donor_send,
        dst_ref=donors.at[me],
        send_sem=donor_sem.at[0],
        recv_sem=donor_sem.at[1],
        device_id={"ins": other},
        device_id_type=MESH,
    )
    donor_copy.start()
    for n in range(per_core):
        remote_in(source_hbm, 1, source, n).start()

    def row_copy(stage, b):
        return pltpu.make_async_remote_copy(
            src_ref=row_send.at[stage],
            dst_ref=row_recv.at[stage, blk],
            send_sem=row_send_sem.at[stage, b],
            recv_sem=row_recv_sem.at[stage, blk],
            device_id={"blk": b, "ins": other},
            device_id_type=MESH,
        )

    def row_arrival(stage, b):
        return pltpu.make_async_remote_copy(
            src_ref=row_send.at[stage],
            dst_ref=row_recv.at[stage, b],
            send_sem=row_send_sem.at[stage, b],
            recv_sem=row_recv_sem.at[stage, b],
            device_id={"blk": b, "ins": other},
            device_id_type=MESH,
        )

    def edge_copy(stage, side):
        return pltpu.make_async_remote_copy(
            src_ref=edge_send.at[stage],
            dst_ref=edge_recv.at[stage, side],
            send_sem=edge_send_sem.at[stage, side],
            recv_sem=edge_recv_sem.at[stage, side],
            device_id={"blk": right if side == 0 else left},
            device_id_type=MESH,
        )

    def send_row(stage):
        for b in range(blocks):
            row_copy(stage, b).start()

    def send_edges(stage):
        for side in range(2):
            edge_copy(stage, side).start()

    flat = {
        id(buffer): buffer.reshape(CHANNELS * pitch, LANES)
        for buffer in (state0, state1, state2, source)
    }

    def load_row(buffer, i):
        return flat[id(buffer)][pl.ds(i, CHANNELS, stride=pitch), :]

    def store_row(buffer, i, value):
        flat[id(buffer)][pl.ds(i, CHANNELS, stride=pitch), :] = value

    lane = lax.broadcasted_iota(jnp.int32, (CHANNELS, LANES), 1)
    first_lane = lane == 0
    last_lane = lane == LANES - 1
    edge_lane = first_lane | last_lane
    pair_index = lane >> 1
    even_lane = (lane & 1) == 0

    def step_row(i):
        return jnp.broadcast_to(dt_ref[pl.ds(me * half + i, 1), :], (CHANNELS, LANES))

    def wall_row(i):
        return jnp.broadcast_to(wall_ref[pl.ds(me * half + i, 1), :], (NINST, LANES))

    def main_pass(current, target, factor):
        def finish(i, total):
            store_row(
                target, i, load_row(state0, i) - (factor * step_row(i)) * total
            )

        def group(t, carry):
            pending, behind = carry
            first = t * 8
            for pair in range(4):
                rows = (first + 2 * pair, first + 2 * pair + 1)
                cells = [load_row(current, i) for i in rows]
                product = jnp.dot(
                    weight_ref[...],
                    split_stack(jnp.concatenate(cells, axis=1)),
                    preferred_element_type=F32,
                )
                for k in range(2):
                    i = rows[k]
                    centre, ahead, back, mc, pc = [
                        product[
                            CHANNELS * g : CHANNELS * (g + 1), LANES * k : LANES * (k + 1)
                        ]
                        for g in range(5)
                    ]
                    before = i - 1
                    if pair == 0 and k == 0:
                        before = jnp.maximum(before, 0)
                    finish(before, pending + ahead)
                    total = centre + behind - load_row(source, i)
                    total += jnp.where(last_lane, 0.0, pltpu.roll(mc, LANES - 1, axis=1))
                    total += jnp.where(first_lane, 0.0, pltpu.roll(pc, 1, axis=1))
                    turbulent = cells[k][CHANNELS - NINST :, :]
                    extra = 2.0 * turbulent * jnp.abs(turbulent) * wall_row(i)
                    pending = jnp.concatenate(
                        [total[: CHANNELS - NINST], total[CHANNELS - NINST :] + extra], axis=0
                    )
                    behind = back
            return pending, behind

        zero = jnp.zeros((CHANNELS, LANES), F32)
        pending, _ = lax.fori_loop(0, half // 8, group, (zero, zero))
        finish(half - 1, pending)

    interface_row = jnp.where(me == 0, half - 1, 0)

    def halo_products(stage):
        for side in range(2):
            edge_copy(stage, side).wait_recv()
        from_left = pltpu.roll(edge_recv[stage, 0], 1, axis=1)
        from_right = pltpu.roll(edge_recv[stage, 1], LANES - 1, axis=1)
        product = jnp.dot(
            weight_ref[3 * CHANNELS :, :],
            split_stack(jnp.concatenate([from_right, from_left], axis=1)),
            preferred_element_type=F32,
        )
        return jnp.where(even_lane, product[:CHANNELS, :LANES], product[CHANNELS:, LANES:])

    def halo_at(halo, i):
        return jnp.where(edge_lane, pltpu.roll(halo, LANES - 1 - 2 * i, axis=1), 0.0)

    def facing_product(stage):
        for b in range(blocks):
            row_arrival(stage, b).wait_recv()
        donor = jnp.concatenate([donors[0], donors[1]], axis=0)
        start = jnp.broadcast_to(donor[:, 0:1], (NINST, LANES))
        shift = start & (LANES - 1)
        block = start >> 7
        small_lane = lax.broadcasted_iota(jnp.int32, (NINST, LANES), 1)
        following = jnp.where(block == blocks - 1, 0, block + 1)
        wanted = jnp.where(small_lane >= shift, block, following)
        index = (small_lane + shift) & (LANES - 1)
        pieces = []
        for v in range(NV):
            piece = jnp.zeros((NINST, LANES), F32)
            for b in range(blocks):
                piece = jnp.where(
                    wanted == b, row_recv[stage, b, v * NINST : (v + 1) * NINST, :], piece
                )
            pieces.append(jnp.take_along_axis(piece, index, axis=1))
        facing = jnp.concatenate(pieces, axis=0)
        matrix = weight_ref[pl.ds(pl.multiple_of(CHANNELS * (1 + me), 16), CHANNELS), :]
        return jnp.dot(matrix, split_stack(facing), preferred_element_type=F32)

    def edge_pass(target, factor, halo, collect):
        def group(t, edges):
            for k in range(8):
                i = t * 8 + k
                value = load_row(target, i)
                if halo is not None:
                    value = value - (factor * step_row(i)) * halo_at(halo, i)
                    store_row(target, i, value)
                if collect:
                    edges = jnp.where(
                        pair_index == i, pltpu.roll(value, 2 * i + 1, axis=1), edges
                    )
            return edges

        return lax.fori_loop(0, half // 8, group, jnp.zeros((CHANNELS, LANES), F32))

    for n in range(per_core):
        local_in(start_hbm, 0, state0, n).wait()
    for n in range(per_core):
        remote_in(start_hbm, 0, state0, n).wait_recv()
    row_send[0] = load_row(state0, interface_row)
    send_row(0)
    edge_send[0] = edge_pass(state0, 0.0, None, True)
    send_edges(0)
    donor_copy.wait_recv()
    for n in range(per_core):
        local_in(source_hbm, 1, source, n).wait()
    for n in range(per_core):
        remote_in(source_hbm, 1, source, n).wait_recv()

    buffers = (state0, state1, state2, state1)
    for stage, factor in enumerate(SEGMENT_FACTORS):
        target = buffers[stage + 1]
        main_pass(buffers[stage], target, factor)
        halo = halo_products(stage)
        facing = facing_product(stage)
        scale = factor * step_row(interface_row)
        value = load_row(target, interface_row) - scale * facing
        store_row(target, interface_row, value)
        if stage < 2:
            row_send[stage + 1] = value - scale * halo_at(halo, interface_row)
            send_row(stage + 1)
        edges = edge_pass(target, factor, halo, stage < 2)
        if stage < 2:
            edge_send[stage + 1] = edges
            send_edges(stage + 1)

    final = buffers[3]

    def local_out(n):
        return pltpu.make_async_copy(
            final.at[:, per_core * me + n, pl.ds(0, half), :],
            out_hbm.at[n, :, my_rows, :],
            local_sem.at[2, n],
        )

    def remote_out(n):
        return pltpu.make_async_remote_copy(
            src_ref=final.at[:, per_core * other + n, pl.ds(0, half), :],
            dst_ref=out_hbm.at[n, :, my_rows, :],
            send_sem=remote_send_sem.at[2, n],
            recv_sem=remote_recv_sem.at[2, n],
            device_id={"ins": other},
            device_id_type=MESH,
        )

    for n in range(per_core):
        remote_out(n).start()
    for n in range(per_core):
        local_out(n).start()
    donor_copy.wait_send()
    for n in range(per_core):
        remote_in(start_hbm, 0, state0, n).wait_send()
        remote_in(source_hbm, 1, source, n).wait_send()
    for stage in range(3):
        for b in range(blocks):
            row_copy(stage, b).wait_send()
        for side in range(2):
            edge_copy(stage, side).wait_send()
    for n in range(per_core):
        local_out(n).wait()
        remote_out(n).wait()


def solution(mesh):
    blocks = mesh.shape["blk"]

    def local(start_state, source_term, time_step, wall_factor, flux_split, stator, rotor):
        per_core, _, rows, _ = start_state.shape
        half = rows // 2
        pitch = half + PITCH_PAD
        state = pltpu.VMEM((NV, NINST, pitch, LANES), F32)
        whole = pl.BlockSpec(memory_space=pltpu.VMEM)
        return pl.pallas_call(
            functools.partial(kernel, blocks, half),
            out_shape=jax.ShapeDtypeStruct(start_state.shape, F32),
            in_specs=[
                pl.BlockSpec(memory_space=pl.ANY),
                pl.BlockSpec(memory_space=pl.ANY),
                whole,
                whole,
                pl.BlockSpec(memory_space=pltpu.SMEM),
                whole,
                whole,
            ],
            out_specs=pl.BlockSpec(memory_space=pl.ANY),
            scratch_shapes=[
                state,
                state,
                state,
                state,
                pltpu.VMEM((5 * CHANNELS, 3 * CHANNELS), BF16),
                pltpu.VMEM((2, per_core, LANES), jnp.int32),
                pltpu.VMEM((per_core, LANES), jnp.int32),
                pltpu.VMEM((3, CHANNELS, LANES), F32),
                pltpu.VMEM((3, blocks, CHANNELS, LANES), F32),
                pltpu.VMEM((3, CHANNELS, LANES), F32),
                pltpu.VMEM((3, 2, CHANNELS, LANES), F32),
                pltpu.SemaphoreType.DMA((3, per_core)),
                pltpu.SemaphoreType.DMA((3, per_core)),
                pltpu.SemaphoreType.DMA((3, per_core)),
                pltpu.SemaphoreType.DMA((2,)),
                pltpu.SemaphoreType.DMA((3, blocks)),
                pltpu.SemaphoreType.DMA((3, blocks)),
                pltpu.SemaphoreType.DMA((3, 2)),
                pltpu.SemaphoreType.DMA((3, 2)),
            ],
            compiler_params=pltpu.CompilerParams(
                collective_id=0, has_side_effects=True, vmem_limit_bytes=48 * 1024 * 1024
            ),
        )(start_state, source_term, time_step, wall_factor, flux_split, stator, rotor)

    return jax.shard_map(
        local,
        mesh=mesh,
        in_specs=(
            P("ins", None, "grp", "blk"),
            P("ins", None, "grp", "blk"),
            P("grp", "blk"),
            P("grp", "blk"),
            P(),
            P("ins", "blk"),
            P("ins", "blk"),
        ),
        out_specs=P("ins", None, "grp", "blk"),
        check_vma=False,
    )
```

```python
import functools
import math

import jax
import jax.numpy as jnp
from jax import lax
from jax.experimental import pallas as pl
from jax.experimental.pallas import tpu as pltpu
from jax.sharding import PartitionSpec as P

NINST = 8
NV = 6
CHANNELS = NINST * NV
LANES = 128
PITCH_PAD = 8
SEGMENT_FACTORS = (1.0 / 3.0, 0.5, 1.0)
MESH = pl.DeviceIdType.MESH
F32 = jnp.float32
BF16 = jnp.bfloat16


def split_stack(values):
    high = values.astype(BF16)
    low = (values - high.astype(F32)).astype(BF16)
    return jnp.concatenate([high, low, high], axis=0)


def build_weights(flux_ref, weight_ref):
    shape = (NINST, 3 * CHANNELS)
    lane = lax.broadcasted_iota(jnp.int32, shape, 1)
    instance = lax.broadcasted_iota(jnp.int32, shape, 0)
    column = (
        lane
        - jnp.where(lane >= CHANNELS, CHANNELS, 0)
        - jnp.where(lane >= 2 * CHANNELS, CHANNELS, 0)
    )
    in_component = column >> 3
    offset = instance - (column & 7)
    spectral = jnp.zeros(shape, F32)
    for d in range(1, NINST):
        value = 0.5 * (-1.0) ** d * math.cos(math.pi * d / NINST) / math.sin(math.pi * d / NINST)
        spectral = jnp.where(offset == d, F32(value), spectral)
        spectral = jnp.where(offset == -d, F32(-value), spectral)
    same = offset == 0

    def flux_row(direction, part, v):
        row = jnp.zeros(shape, F32)
        for w in range(NV):
            row = jnp.where(in_component == w, flux_ref[direction, v, part, w], row)
        return row

    rows = [[], [], [], [], []]
    for v in range(NV):
        pa, ma = flux_row(0, 0, v), flux_row(0, 1, v)
        pc, mc = flux_row(1, 0, v), flux_row(1, 1, v)
        centre = jnp.where(same, pa - ma + pc - mc, 0.0) + jnp.where(
            in_component == v, spectral, 0.0
        )
        rows[0].append(centre)
        for place, matrix in ((1, ma), (2, -pa), (3, mc), (4, -pc)):
            rows[place].append(jnp.where(same, matrix, 0.0))
    flat = [row for group in rows for row in group]
    for k in range(0, len(flat), 2):
        value = jnp.concatenate([flat[k], flat[k + 1]], axis=0)
        high = value.astype(BF16).astype(F32)
        wide = lax.broadcasted_iota(jnp.int32, value.shape, 1)
        weight_ref[k * 8 : k * 8 + 16, :] = jnp.where(
            wide < 2 * CHANNELS, high, value - high
        ).astype(BF16)


def kernel(
    blocks,
    half,
    start_hbm,
    source_hbm,
    dt_hbm,
    wall_hbm,
    flux_ref,
    stator_hbm,
    rotor_hbm,
    out_hbm,
    dt_ref,
    wall_ref,
    stator_ref,
    rotor_ref,
    small_sem,
    state0,
    state1,
    state2,
    source,
    weight_ref,
    donors,
    donor_send,
    row_send,
    row_recv,
    edge_send,
    edge_recv,
    local_sem,
    remote_send_sem,
    remote_recv_sem,
    donor_sem,
    row_send_sem,
    row_recv_sem,
    edge_send_sem,
    edge_recv_sem,
):
    me = lax.axis_index("ins")
    blk = lax.axis_index("blk")
    other = 1 - me
    per_core = start_hbm.shape[0]
    pitch = half + PITCH_PAD
    right = lax.rem(blk + 1, blocks)
    left = lax.rem(blk + blocks - 1, blocks)
    my_rows = pl.ds(pl.multiple_of(me * half, 8), half)
    other_rows = pl.ds(pl.multiple_of(other * half, 8), half)

    def local_in(array, place, buffer, n):
        return pltpu.make_async_copy(
            array.at[n, :, my_rows, :],
            buffer.at[:, per_core * me + n, pl.ds(0, half), :],
            local_sem.at[place, n],
        )

    def remote_in(array, place, buffer, n):
        return pltpu.make_async_remote_copy(
            src_ref=array.at[n, :, other_rows, :],
            dst_ref=buffer.at[:, per_core * me + n, pl.ds(0, half), :],
            send_sem=remote_send_sem.at[place, n],
            recv_sem=remote_recv_sem.at[place, n],
            device_id={"ins": other},
            device_id_type=MESH,
        )

    for n in range(per_core):
        local_in(start_hbm, 0, state0, n).start()

    small = [
        pltpu.make_async_copy(stator_hbm, stator_ref, small_sem.at[0]),
        pltpu.make_async_copy(rotor_hbm, rotor_ref, small_sem.at[1]),
        pltpu.make_async_copy(dt_hbm.at[my_rows, :], dt_ref, small_sem.at[2]),
        pltpu.make_async_copy(wall_hbm.at[my_rows, :], wall_ref, small_sem.at[3]),
    ]
    for copy in small:
        copy.start()
    barrier = pltpu.get_barrier_semaphore()
    for b in range(blocks):
        pl.semaphore_signal(barrier, inc=1, device_id={"blk": b, "ins": other}, device_id_type=MESH)
    for b in (left, right):
        pl.semaphore_signal(barrier, inc=1, device_id={"blk": b}, device_id_type=MESH)
    for n in range(per_core):
        local_in(source_hbm, 1, source, n).start()
    build_weights(flux_ref, weight_ref)
    for copy in small:
        copy.wait()
    stator = stator_ref[...]
    rotor = rotor_ref[...]
    donors[me] = jnp.where(me == 0, stator, rotor)
    donor_send[...] = jnp.where(me == 0, rotor, stator)
    pl.semaphore_wait(barrier, blocks + 2)

    for n in range(per_core):
        remote_in(start_hbm, 0, state0, n).start()
    donor_copy = pltpu.make_async_remote_copy(
        src_ref=donor_send,
        dst_ref=donors.at[me],
        send_sem=donor_sem.at[0],
        recv_sem=donor_sem.at[1],
        device_id={"ins": other},
        device_id_type=MESH,
    )
    donor_copy.start()
    for n in range(per_core):
        remote_in(source_hbm, 1, source, n).start()

    def row_copy(stage, b):
        return pltpu.make_async_remote_copy(
            src_ref=row_send.at[stage],
            dst_ref=row_recv.at[stage, blk],
            send_sem=row_send_sem.at[stage, b],
            recv_sem=row_recv_sem.at[stage, blk],
            device_id={"blk": b, "ins": other},
            device_id_type=MESH,
        )

    def row_arrival(stage, b):
        return pltpu.make_async_remote_copy(
            src_ref=row_send.at[stage],
            dst_ref=row_recv.at[stage, b],
            send_sem=row_send_sem.at[stage, b],
            recv_sem=row_recv_sem.at[stage, b],
            device_id={"blk": b, "ins": other},
            device_id_type=MESH,
        )

    def edge_copy(stage, side):
        return pltpu.make_async_remote_copy(
            src_ref=edge_send.at[stage],
            dst_ref=edge_recv.at[stage, side],
            send_sem=edge_send_sem.at[stage, side],
            recv_sem=edge_recv_sem.at[stage, side],
            device_id={"blk": right if side == 0 else left},
            device_id_type=MESH,
        )

    def send_row(stage):
        for b in range(blocks):
            row_copy(stage, b).start()

    def send_edges(stage):
        for side in range(2):
            edge_copy(stage, side).start()

    flat = {
        id(buffer): buffer.reshape(CHANNELS * pitch, LANES)
        for buffer in (state0, state1, state2, source)
    }

    def load_row(buffer, i):
        return flat[id(buffer)][pl.ds(i, CHANNELS, stride=pitch), :]

    def store_row(buffer, i, value):
        flat[id(buffer)][pl.ds(i, CHANNELS, stride=pitch), :] = value

    lane = lax.broadcasted_iota(jnp.int32, (CHANNELS, LANES), 1)
    first_lane = lane == 0
    last_lane = lane == LANES - 1
    edge_lane = first_lane | last_lane
    pair_index = lane >> 1
    even_lane = (lane & 1) == 0

    def step_row(i):
        return jnp.broadcast_to(dt_ref[pl.ds(i, 1), :], (CHANNELS, LANES))

    def wall_row(i):
        return jnp.broadcast_to(wall_ref[pl.ds(i, 1), :], (NINST, LANES))

    def main_pass(current, target, factor):
        def finish(i, total):
            store_row(
                target, i, load_row(state0, i) - (factor * step_row(i)) * total
            )

        def group(t, carry):
            pending, behind = carry
            first = t * 8
            for pair in range(4):
                rows = (first + 2 * pair, first + 2 * pair + 1)
                cells = [load_row(current, i) for i in rows]
                product = jnp.dot(
                    weight_ref[...],
                    split_stack(jnp.concatenate(cells, axis=1)),
                    preferred_element_type=F32,
                )
                for k in range(2):
                    i = rows[k]
                    centre, ahead, back, mc, pc = [
                        product[
                            CHANNELS * g : CHANNELS * (g + 1), LANES * k : LANES * (k + 1)
                        ]
                        for g in range(5)
                    ]
                    before = i - 1
                    if pair == 0 and k == 0:
                        before = jnp.maximum(before, 0)
                    finish(before, pending + ahead)
                    total = centre + behind - load_row(source, i)
                    total += jnp.where(last_lane, 0.0, pltpu.roll(mc, LANES - 1, axis=1))
                    total += jnp.where(first_lane, 0.0, pltpu.roll(pc, 1, axis=1))
                    turbulent = cells[k][CHANNELS - NINST :, :]
                    extra = 2.0 * turbulent * jnp.abs(turbulent) * wall_row(i)
                    pending = jnp.concatenate(
                        [total[: CHANNELS - NINST], total[CHANNELS - NINST :] + extra], axis=0
                    )
                    behind = back
            return pending, behind

        zero = jnp.zeros((CHANNELS, LANES), F32)
        pending, _ = lax.fori_loop(0, half // 8, group, (zero, zero))
        finish(half - 1, pending)

    interface_row = jnp.where(me == 0, half - 1, 0)

    def halo_products(stage):
        for side in range(2):
            edge_copy(stage, side).wait_recv()
        from_left = pltpu.roll(edge_recv[stage, 0], 1, axis=1)
        from_right = pltpu.roll(edge_recv[stage, 1], LANES - 1, axis=1)
        product = jnp.dot(
            weight_ref[3 * CHANNELS :, :],
            split_stack(jnp.concatenate([from_right, from_left], axis=1)),
            preferred_element_type=F32,
        )
        return jnp.where(even_lane, product[:CHANNELS, :LANES], product[CHANNELS:, LANES:])

    def halo_at(halo, i):
        return jnp.where(edge_lane, pltpu.roll(halo, LANES - 1 - 2 * i, axis=1), 0.0)

    def facing_product(stage):
        for b in range(blocks):
            row_arrival(stage, b).wait_recv()
        donor = jnp.concatenate([donors[0], donors[1]], axis=0)
        start = jnp.broadcast_to(donor[:, 0:1], (NINST, LANES))
        shift = start & (LANES - 1)
        block = start >> 7
        small_lane = lax.broadcasted_iota(jnp.int32, (NINST, LANES), 1)
        following = jnp.where(block == blocks - 1, 0, block + 1)
        wanted = jnp.where(small_lane >= shift, block, following)
        index = (small_lane + shift) & (LANES - 1)
        pieces = []
        for v in range(NV):
            piece = jnp.zeros((NINST, LANES), F32)
            for b in range(blocks):
                piece = jnp.where(
                    wanted == b, row_recv[stage, b, v * NINST : (v + 1) * NINST, :], piece
                )
            pieces.append(jnp.take_along_axis(piece, index, axis=1))
        facing = jnp.concatenate(pieces, axis=0)
        matrix = weight_ref[pl.ds(pl.multiple_of(CHANNELS * (1 + me), 16), CHANNELS), :]
        return jnp.dot(matrix, split_stack(facing), preferred_element_type=F32)

    def edge_pass(target, factor, halo, collect):
        def group(t, edges):
            for k in range(8):
                i = t * 8 + k
                value = load_row(target, i)
                if halo is not None:
                    value = value - (factor * step_row(i)) * halo_at(halo, i)
                    store_row(target, i, value)
                if collect:
                    edges = jnp.where(
                        pair_index == i, pltpu.roll(value, 2 * i + 1, axis=1), edges
                    )
            return edges

        return lax.fori_loop(0, half // 8, group, jnp.zeros((CHANNELS, LANES), F32))

    for n in range(per_core):
        local_in(start_hbm, 0, state0, n).wait()
    for n in range(per_core):
        remote_in(start_hbm, 0, state0, n).wait_recv()
    row_send[0] = load_row(state0, interface_row)
    send_row(0)
    edge_send[0] = edge_pass(state0, 0.0, None, True)
    send_edges(0)
    donor_copy.wait_recv()
    for n in range(per_core):
        local_in(source_hbm, 1, source, n).wait()
    for n in range(per_core):
        remote_in(source_hbm, 1, source, n).wait_recv()

    buffers = (state0, state1, state2, state1)
    for stage, factor in enumerate(SEGMENT_FACTORS):
        target = buffers[stage + 1]
        main_pass(buffers[stage], target, factor)
        halo = halo_products(stage)
        facing = facing_product(stage)
        scale = factor * step_row(interface_row)
        value = load_row(target, interface_row) - scale * facing
        store_row(target, interface_row, value)
        if stage < 2:
            row_send[stage + 1] = value - scale * halo_at(halo, interface_row)
            send_row(stage + 1)
        edges = edge_pass(target, factor, halo, stage < 2)
        if stage < 2:
            edge_send[stage + 1] = edges
            send_edges(stage + 1)

    final = buffers[3]

    def local_out(n):
        return pltpu.make_async_copy(
            final.at[:, per_core * me + n, pl.ds(0, half), :],
            out_hbm.at[n, :, my_rows, :],
            local_sem.at[2, n],
        )

    def remote_out(n):
        return pltpu.make_async_remote_copy(
            src_ref=final.at[:, per_core * other + n, pl.ds(0, half), :],
            dst_ref=out_hbm.at[n, :, my_rows, :],
            send_sem=remote_send_sem.at[2, n],
            recv_sem=remote_recv_sem.at[2, n],
            device_id={"ins": other},
            device_id_type=MESH,
        )

    for n in range(per_core):
        remote_out(n).start()
    for n in range(per_core):
        local_out(n).start()
    donor_copy.wait_send()
    for n in range(per_core):
        remote_in(start_hbm, 0, state0, n).wait_send()
        remote_in(source_hbm, 1, source, n).wait_send()
    for stage in range(3):
        for b in range(blocks):
            row_copy(stage, b).wait_send()
        for side in range(2):
            edge_copy(stage, side).wait_send()
    for n in range(per_core):
        local_out(n).wait()
        remote_out(n).wait()


def solution(mesh):
    blocks = mesh.shape["blk"]

    def local(start_state, source_term, time_step, wall_factor, flux_split, stator, rotor):
        per_core, _, rows, _ = start_state.shape
        half = rows // 2
        pitch = half + PITCH_PAD
        state = pltpu.VMEM((NV, NINST, pitch, LANES), F32)
        hbm = pl.BlockSpec(memory_space=pltpu.HBM)
        return pl.pallas_call(
            functools.partial(kernel, blocks, half),
            out_shape=pltpu.VMEM(start_state.shape, F32),
            in_specs=[
                hbm,
                hbm,
                hbm,
                hbm,
                pl.BlockSpec(memory_space=pltpu.SMEM),
                hbm,
                hbm,
            ],
            out_specs=pl.BlockSpec(memory_space=pl.ANY),
            scratch_shapes=[
                pltpu.VMEM((half, LANES), F32),
                pltpu.VMEM((half, LANES), F32),
                pltpu.VMEM((per_core, LANES), jnp.int32),
                pltpu.VMEM((per_core, LANES), jnp.int32),
                pltpu.SemaphoreType.DMA((4,)),
                state,
                state,
                state,
                state,
                pltpu.VMEM((5 * CHANNELS, 3 * CHANNELS), BF16),
                pltpu.VMEM((2, per_core, LANES), jnp.int32),
                pltpu.VMEM((per_core, LANES), jnp.int32),
                pltpu.VMEM((3, CHANNELS, LANES), F32),
                pltpu.VMEM((3, blocks, CHANNELS, LANES), F32),
                pltpu.VMEM((3, CHANNELS, LANES), F32),
                pltpu.VMEM((3, 2, CHANNELS, LANES), F32),
                pltpu.SemaphoreType.DMA((3, per_core)),
                pltpu.SemaphoreType.DMA((3, per_core)),
                pltpu.SemaphoreType.DMA((3, per_core)),
                pltpu.SemaphoreType.DMA((2,)),
                pltpu.SemaphoreType.DMA((3, blocks)),
                pltpu.SemaphoreType.DMA((3, blocks)),
                pltpu.SemaphoreType.DMA((3, 2)),
                pltpu.SemaphoreType.DMA((3, 2)),
            ],
            compiler_params=pltpu.CompilerParams(
                collective_id=0, has_side_effects=True, vmem_limit_bytes=56 * 1024 * 1024
            ),
        )(start_state, source_term, time_step, wall_factor, flux_split.transpose(0, 2, 1, 3), stator, rotor)

    return jax.shard_map(
        local,
        mesh=mesh,
        in_specs=(
            P("ins", None, "grp", "blk"),
            P("ins", None, "grp", "blk"),
            P("grp", "blk"),
            P("grp", "blk"),
            P(),
            P("ins", "blk"),
            P("ins", "blk"),
        ),
        out_specs=P("ins", None, "grp", "blk"),
        check_vma=False,
    )
```

```python
import functools
import math

import jax
import jax.numpy as jnp
from jax import lax
from jax.experimental import pallas as pl
from jax.experimental.pallas import tpu as pltpu
from jax.sharding import PartitionSpec as P

NINST = 8
NV = 6
CHANNELS = NINST * NV
LANES = 128
PITCH_PAD = 8
GROUP = 16
SEGMENT_FACTORS = (1.0 / 3.0, 0.5, 1.0)
MESH = pl.DeviceIdType.MESH
F32 = jnp.float32
BF16 = jnp.bfloat16


def split_stack(values):
    high = values.astype(BF16)
    low = (values - high.astype(F32)).astype(BF16)
    return jnp.concatenate([high, low, high], axis=0)


def build_weights(flux_ref, weight_ref):
    shape = (NINST, 3 * CHANNELS)
    lane = lax.broadcasted_iota(jnp.int32, shape, 1)
    instance = lax.broadcasted_iota(jnp.int32, shape, 0)
    column = (
        lane
        - jnp.where(lane >= CHANNELS, CHANNELS, 0)
        - jnp.where(lane >= 2 * CHANNELS, CHANNELS, 0)
    )
    in_component = column >> 3
    offset = instance - (column & 7)
    spectral = jnp.zeros(shape, F32)
    for d in range(1, NINST):
        value = 0.5 * (-1.0) ** d * math.cos(math.pi * d / NINST) / math.sin(math.pi * d / NINST)
        spectral = jnp.where(offset == d, F32(value), spectral)
        spectral = jnp.where(offset == -d, F32(-value), spectral)
    same = offset == 0

    def flux_row(direction, part, v):
        row = jnp.zeros(shape, F32)
        for w in range(NV):
            row = jnp.where(in_component == w, flux_ref[direction, v, part, w], row)
        return row

    rows = [[], [], [], [], []]
    for v in range(NV):
        pa, ma = flux_row(0, 0, v), flux_row(0, 1, v)
        pc, mc = flux_row(1, 0, v), flux_row(1, 1, v)
        centre = jnp.where(same, pa - ma + pc - mc, 0.0) + jnp.where(
            in_component == v, spectral, 0.0
        )
        rows[0].append(centre)
        for place, matrix in ((1, ma), (2, -pa), (3, mc), (4, -pc)):
            rows[place].append(jnp.where(same, matrix, 0.0))
    flat = [row for group in rows for row in group]
    for k in range(0, len(flat), 2):
        value = jnp.concatenate([flat[k], flat[k + 1]], axis=0)
        high = value.astype(BF16).astype(F32)
        wide = lax.broadcasted_iota(jnp.int32, value.shape, 1)
        weight_ref[k * 8 : k * 8 + 16, :] = jnp.where(
            wide < 2 * CHANNELS, high, value - high
        ).astype(BF16)


def kernel(
    blocks,
    half,
    start_hbm,
    source_hbm,
    dt_hbm,
    wall_hbm,
    flux_ref,
    stator_hbm,
    rotor_hbm,
    out_hbm,
    dt_ref,
    wall_ref,
    stator_ref,
    rotor_ref,
    small_sem,
    own,
    first_edge_send,
    first_edge_recv,
    first_edge_send_sem,
    first_edge_recv_sem,
    first_send,
    first_recv,
    first_sem,
    first_send_sem,
    first_recv_sem,
    state0,
    state1,
    state2,
    source,
    weight_ref,
    donors,
    donor_send,
    row_send,
    row_recv,
    edge_send,
    edge_recv,
    local_sem,
    remote_send_sem,
    remote_recv_sem,
    donor_sem,
    row_send_sem,
    row_recv_sem,
    edge_send_sem,
    edge_recv_sem,
):
    me = lax.axis_index("ins")
    blk = lax.axis_index("blk")
    other = 1 - me
    per_core = start_hbm.shape[0]
    pitch = half + PITCH_PAD
    right = lax.rem(blk + 1, blocks)
    left = lax.rem(blk + blocks - 1, blocks)
    my_rows = pl.ds(pl.multiple_of(me * half, 8), half)
    other_rows = pl.ds(pl.multiple_of(other * half, 8), half)

    def local_in(array, place, buffer, n):
        return pltpu.make_async_copy(
            array.at[n, :, my_rows, :],
            buffer.at[:, per_core * me + n, pl.ds(0, half), :],
            local_sem.at[place, n],
        )

    def remote_in(array, place, buffer, n):
        return pltpu.make_async_remote_copy(
            src_ref=array.at[n, :, other_rows, :],
            dst_ref=buffer.at[:, per_core * me + n, pl.ds(0, half), :],
            send_sem=remote_send_sem.at[place, n],
            recv_sem=remote_recv_sem.at[place, n],
            device_id={"ins": other},
            device_id_type=MESH,
        )

    first_copy = pltpu.make_async_copy(
        start_hbm, own.at[:, :, pl.ds(0, 2 * half), :], first_sem
    )
    first_copy.start()
    small = [
        pltpu.make_async_copy(stator_hbm, stator_ref, small_sem.at[0]),
        pltpu.make_async_copy(rotor_hbm, rotor_ref, small_sem.at[1]),
        pltpu.make_async_copy(dt_hbm.at[my_rows, :], dt_ref, small_sem.at[2]),
        pltpu.make_async_copy(wall_hbm.at[my_rows, :], wall_ref, small_sem.at[3]),
    ]
    for copy in small:
        copy.start()
    barrier = pltpu.get_barrier_semaphore()
    for b in range(blocks):
        pl.semaphore_signal(barrier, inc=1, device_id={"blk": b, "ins": other}, device_id_type=MESH)
    for d in range(1, blocks):
        pl.semaphore_signal(
            barrier, inc=1, device_id={"blk": lax.rem(blk + d, blocks)}, device_id_type=MESH
        )
    for n in range(per_core):
        local_in(start_hbm, 0, state0, n).start()
    for n in range(per_core):
        local_in(source_hbm, 1, source, n).start()
    build_weights(flux_ref, weight_ref)
    for copy in small:
        copy.wait()
    stator = stator_ref[...]
    rotor = rotor_ref[...]
    donors[me] = jnp.where(me == 0, stator, rotor)
    donor_send[...] = jnp.where(me == 0, rotor, stator)
    first_copy.wait()
    own_channels = per_core * NV
    own_pitch = 2 * half + PITCH_PAD
    flat_own = own.reshape(own_channels * own_pitch, LANES)

    def own_row(i):
        return flat_own[pl.ds(i, own_channels, stride=own_pitch), :]

    first_send[0] = own_row(half)
    first_send[1] = own_row(half - 1)
    first_recv[blk, me] = first_send[me]
    own_pair = lax.broadcasted_iota(jnp.int32, (own_channels, LANES), 1) >> 1

    def collect_own(t, edges):
        low, high = edges
        for k in range(8):
            i = t * 8 + k
            low = jnp.where(own_pair == i, pltpu.roll(own_row(i), 2 * i + 1, axis=1), low)
            high = jnp.where(
                own_pair == i, pltpu.roll(own_row(half + i), 2 * i + 1, axis=1), high
            )
        return low, high

    nothing = jnp.zeros((own_channels, LANES), F32)
    low_edges, high_edges = lax.fori_loop(0, half // 8, collect_own, (nothing, nothing))
    first_edge_send[0] = low_edges
    first_edge_send[1] = high_edges
    pl.semaphore_wait(barrier, 2 * blocks - 1)

    donor_copy = pltpu.make_async_remote_copy(
        src_ref=donor_send,
        dst_ref=donors.at[me],
        send_sem=donor_sem.at[0],
        recv_sem=donor_sem.at[1],
        device_id={"ins": other},
        device_id_type=MESH,
    )
    donor_copy.start()

    def first_edge_copy(core, side):
        return pltpu.make_async_remote_copy(
            src_ref=first_edge_send.at[core],
            dst_ref=first_edge_recv.at[side, me],
            send_sem=first_edge_send_sem.at[core, side],
            recv_sem=first_edge_recv_sem.at[side, me],
            device_id={"blk": right if side == 0 else left, "ins": core},
            device_id_type=MESH,
        )

    def first_edge_arrival(core, side):
        return pltpu.make_async_remote_copy(
            src_ref=first_edge_send.at[core],
            dst_ref=first_edge_recv.at[side, core],
            send_sem=first_edge_send_sem.at[core, side],
            recv_sem=first_edge_recv_sem.at[side, core],
            device_id={"blk": right if side == 0 else left, "ins": core},
            device_id_type=MESH,
        )

    first_edges = [(core, side) for core in range(2) for side in range(2)]

    def first_row_copy(core, b):
        return pltpu.make_async_remote_copy(
            src_ref=first_send.at[core],
            dst_ref=first_recv.at[blk, me],
            send_sem=first_send_sem.at[core, b],
            recv_sem=first_recv_sem.at[me, blk],
            device_id={"blk": b, "ins": core},
            device_id_type=MESH,
        )

    def first_row_arrival(core, b):
        return pltpu.make_async_remote_copy(
            src_ref=first_send.at[core],
            dst_ref=first_recv.at[b, core],
            send_sem=first_send_sem.at[core, b],
            recv_sem=first_recv_sem.at[core, b],
            device_id={"blk": b, "ins": core},
            device_id_type=MESH,
        )

    first_peers = [(me, lax.rem(blk + d, blocks)) for d in range(1, blocks)]
    first_peers += [(other, lax.rem(blk + d, blocks)) for d in range(blocks)]
    for core, b in first_peers:
        first_row_copy(core, b).start()
    for core, side in first_edges:
        first_edge_copy(core, side).start()
    for n in range(per_core):
        remote_in(start_hbm, 0, state0, n).start()
    for n in range(per_core):
        remote_in(source_hbm, 1, source, n).start()

    def row_copy(stage, b):
        return pltpu.make_async_remote_copy(
            src_ref=row_send.at[stage],
            dst_ref=row_recv.at[stage, blk],
            send_sem=row_send_sem.at[stage, b],
            recv_sem=row_recv_sem.at[stage, blk],
            device_id={"blk": b, "ins": other},
            device_id_type=MESH,
        )

    def row_arrival(stage, b):
        return pltpu.make_async_remote_copy(
            src_ref=row_send.at[stage],
            dst_ref=row_recv.at[stage, b],
            send_sem=row_send_sem.at[stage, b],
            recv_sem=row_recv_sem.at[stage, b],
            device_id={"blk": b, "ins": other},
            device_id_type=MESH,
        )

    def edge_copy(stage, side):
        return pltpu.make_async_remote_copy(
            src_ref=edge_send.at[stage],
            dst_ref=edge_recv.at[stage, side],
            send_sem=edge_send_sem.at[stage, side],
            recv_sem=edge_recv_sem.at[stage, side],
            device_id={"blk": right if side == 0 else left},
            device_id_type=MESH,
        )

    def send_row(stage):
        for b in range(blocks):
            row_copy(stage, b).start()

    def send_edges(stage):
        for side in range(2):
            edge_copy(stage, side).start()

    flat = {
        id(buffer): buffer.reshape(CHANNELS * pitch, LANES)
        for buffer in (state0, state1, state2, source)
    }

    def load_row(buffer, i):
        return flat[id(buffer)][pl.ds(i, CHANNELS, stride=pitch), :]

    def store_row(buffer, i, value):
        flat[id(buffer)][pl.ds(i, CHANNELS, stride=pitch), :] = value

    lane = lax.broadcasted_iota(jnp.int32, (CHANNELS, LANES), 1)
    first_lane = lane == 0
    last_lane = lane == LANES - 1
    edge_lane = first_lane | last_lane
    pair_index = lane >> 1
    even_lane = (lane & 1) == 0

    def step_row(i):
        return jnp.broadcast_to(dt_ref[pl.ds(i, 1), :], (CHANNELS, LANES))

    def wall_row(i):
        return jnp.broadcast_to(wall_ref[pl.ds(i, 1), :], (NINST, LANES))

    def main_pass(current, target, factor, halo, collect):
        def finish(i, total, edges):
            value = load_row(state0, i) - (factor * step_row(i)) * total
            store_row(target, i, value)
            if collect:
                edges = jnp.where(pair_index == i, pltpu.roll(value, 2 * i + 1, axis=1), edges)
            return edges

        def corrected(i):
            value = load_row(current, i)
            return value if halo is None else value - halo_at(halo, i)

        def group(t, carry):
            pending, behind, edges = carry
            first = t * GROUP
            for pair in range(GROUP // 2):
                rows = (first + 2 * pair, first + 2 * pair + 1)
                cells = [corrected(i) for i in rows]
                product = jnp.dot(
                    weight_ref[...],
                    split_stack(jnp.concatenate(cells, axis=1)),
                    preferred_element_type=F32,
                )
                for k in range(2):
                    i = rows[k]
                    centre, ahead, back, mc, pc = [
                        product[
                            CHANNELS * g : CHANNELS * (g + 1), LANES * k : LANES * (k + 1)
                        ]
                        for g in range(5)
                    ]
                    before = i - 1
                    if pair == 0 and k == 0:
                        before = jnp.maximum(before, 0)
                    edges = finish(before, pending + ahead, edges)
                    total = centre + behind - load_row(source, i)
                    total += jnp.where(last_lane, 0.0, pltpu.roll(mc, LANES - 1, axis=1))
                    total += jnp.where(first_lane, 0.0, pltpu.roll(pc, 1, axis=1))
                    turbulent = cells[k][CHANNELS - NINST :, :]
                    extra = 2.0 * turbulent * jnp.abs(turbulent) * wall_row(i)
                    pending = jnp.concatenate(
                        [total[: CHANNELS - NINST], total[CHANNELS - NINST :] + extra], axis=0
                    )
                    behind = back
            return pending, behind, edges

        zero = jnp.zeros((CHANNELS, LANES), F32)
        pending, _, edges = lax.fori_loop(0, half // GROUP, group, (zero, zero, zero))
        return finish(half - 1, pending, edges)

    interface_row = jnp.where(me == 0, half - 1, 0)

    def halo_products(stage):
        if stage == 0:
            for core, side in first_edges:
                first_edge_arrival(core, side).wait_recv()
            flat_edges = first_edge_recv.reshape(2 * CHANNELS, LANES)
            arrived = [
                jnp.concatenate(
                    [
                        flat_edges[pl.ds(side * CHANNELS + v, NINST, stride=NV), :]
                        for v in range(NV)
                    ],
                    axis=0,
                )
                for side in range(2)
            ]
        else:
            for side in range(2):
                edge_copy(stage - 1, side).wait_recv()
            arrived = [edge_recv[stage - 1, side] for side in range(2)]
        from_left = pltpu.roll(arrived[0], 1, axis=1)
        from_right = pltpu.roll(arrived[1], LANES - 1, axis=1)
        product = jnp.dot(
            weight_ref[3 * CHANNELS :, :],
            split_stack(jnp.concatenate([from_right, from_left], axis=1)),
            preferred_element_type=F32,
        )
        return jnp.where(even_lane, product[:CHANNELS, :LANES], product[CHANNELS:, LANES:])

    def halo_at(halo, i):
        return jnp.where(edge_lane, pltpu.roll(halo, LANES - 1 - 2 * i, axis=1), 0.0)

    def facing_product(stage):
        if stage == 0:
            for core, b in first_peers:
                first_row_arrival(core, b).wait_recv()
        else:
            for b in range(blocks):
                row_arrival(stage - 1, b).wait_recv()
        flat_recv = first_recv.reshape(blocks * CHANNELS, LANES)

        def arrived(b, v):
            if stage == 0:
                return flat_recv[pl.ds(b * CHANNELS + v, NINST, stride=NV), :]
            return row_recv[stage - 1, b, v * NINST : (v + 1) * NINST, :]

        donor = jnp.concatenate([donors[0], donors[1]], axis=0)
        start = jnp.broadcast_to(donor[:, 0:1], (NINST, LANES))
        shift = start & (LANES - 1)
        block = start >> 7
        small_lane = lax.broadcasted_iota(jnp.int32, (NINST, LANES), 1)
        following = jnp.where(block == blocks - 1, 0, block + 1)
        wanted = jnp.where(small_lane >= shift, block, following)
        index = (small_lane + shift) & (LANES - 1)
        pieces = []
        for v in range(NV):
            piece = jnp.zeros((NINST, LANES), F32)
            for b in range(blocks):
                piece = jnp.where(wanted == b, arrived(b, v), piece)
            pieces.append(jnp.take_along_axis(piece, index, axis=1))
        facing = jnp.concatenate(pieces, axis=0)
        matrix = weight_ref[pl.ds(pl.multiple_of(CHANNELS * (1 + me), 16), CHANNELS), :]
        return jnp.dot(matrix, split_stack(facing), preferred_element_type=F32)

    def compact_steps(t, steps):
        for k in range(8):
            i = t * 8 + k
            row = jnp.broadcast_to(dt_ref[pl.ds(i, 1), :], (NINST, LANES))
            steps = jnp.where(small_pair == i, pltpu.roll(row, 2 * i + 1, axis=1), steps)
        return steps

    small_pair = lax.broadcasted_iota(jnp.int32, (NINST, LANES), 1) >> 1
    edge_steps = lax.fori_loop(0, half // 8, compact_steps, jnp.zeros((NINST, LANES), F32))
    edge_steps = jnp.concatenate([edge_steps] * NV, axis=0)

    def last_pass(target, halo):
        def group(t, carry):
            for k in range(8):
                i = t * 8 + k
                store_row(target, i, load_row(target, i) - halo_at(halo, i))
            return carry

        lax.fori_loop(0, half // 8, group, 0)

    for n in range(per_core):
        local_in(start_hbm, 0, state0, n).wait()
    for n in range(per_core):
        remote_in(start_hbm, 0, state0, n).wait_recv()
    donor_copy.wait_recv()
    for n in range(per_core):
        local_in(source_hbm, 1, source, n).wait()
    for n in range(per_core):
        remote_in(source_hbm, 1, source, n).wait_recv()

    buffers = (state0, state1, state2, state1)
    halo = None
    for stage, factor in enumerate(SEGMENT_FACTORS):
        target = buffers[stage + 1]
        edges = main_pass(buffers[stage], target, factor, halo, stage < 2)
        halo = (factor * edge_steps) * halo_products(stage)
        change = (factor * step_row(interface_row)) * facing_product(stage)
        value = load_row(target, interface_row) - change
        store_row(target, interface_row, value)
        if stage < 2:
            row_send[stage] = value - halo_at(halo, interface_row)
            send_row(stage)
            corner = pltpu.roll(change, 2 * interface_row + 1, axis=1)
            edge_send[stage] = (
                edges - halo - jnp.where(pair_index == interface_row, corner, 0.0)
            )
            send_edges(stage)
    last_pass(buffers[3], halo)

    final = buffers[3]

    def local_out(n):
        return pltpu.make_async_copy(
            final.at[:, per_core * me + n, pl.ds(0, half), :],
            out_hbm.at[n, :, my_rows, :],
            local_sem.at[2, n],
        )

    def remote_out(n):
        return pltpu.make_async_remote_copy(
            src_ref=final.at[:, per_core * other + n, pl.ds(0, half), :],
            dst_ref=out_hbm.at[n, :, my_rows, :],
            send_sem=remote_send_sem.at[2, n],
            recv_sem=remote_recv_sem.at[2, n],
            device_id={"ins": other},
            device_id_type=MESH,
        )

    for n in range(per_core):
        remote_out(n).start()
    for n in range(per_core):
        local_out(n).start()
    donor_copy.wait_send()
    for n in range(per_core):
        remote_in(start_hbm, 0, state0, n).wait_send()
        remote_in(source_hbm, 1, source, n).wait_send()
    for core, b in first_peers:
        first_row_copy(core, b).wait_send()
    for core, side in first_edges:
        first_edge_copy(core, side).wait_send()
    for stage in range(2):
        for b in range(blocks):
            row_copy(stage, b).wait_send()
        for side in range(2):
            edge_copy(stage, side).wait_send()
    for n in range(per_core):
        local_out(n).wait()
        remote_out(n).wait()


def solution(mesh):
    blocks = mesh.shape["blk"]

    def local(start_state, source_term, time_step, wall_factor, flux_split, stator, rotor):
        per_core, _, rows, _ = start_state.shape
        half = rows // 2
        pitch = half + PITCH_PAD
        state = pltpu.VMEM((NV, NINST, pitch, LANES), F32)
        hbm = pl.BlockSpec(memory_space=pltpu.HBM)
        return pl.pallas_call(
            functools.partial(kernel, blocks, half),
            out_shape=pltpu.VMEM(start_state.shape, F32),
            in_specs=[
                hbm,
                hbm,
                hbm,
                hbm,
                pl.BlockSpec(memory_space=pltpu.SMEM),
                hbm,
                hbm,
            ],
            out_specs=pl.BlockSpec(memory_space=pl.ANY),
            scratch_shapes=[
                pltpu.VMEM((half, LANES), F32),
                pltpu.VMEM((half, LANES), F32),
                pltpu.VMEM((per_core, LANES), jnp.int32),
                pltpu.VMEM((per_core, LANES), jnp.int32),
                pltpu.SemaphoreType.DMA((4,)),
                pltpu.VMEM((per_core, NV, rows + PITCH_PAD, LANES), F32),
                pltpu.VMEM((2, per_core * NV, LANES), F32),
                pltpu.VMEM((2, 2, per_core * NV, LANES), F32),
                pltpu.SemaphoreType.DMA((2, 2)),
                pltpu.SemaphoreType.DMA((2, 2)),
                pltpu.VMEM((2, per_core * NV, LANES), F32),
                pltpu.VMEM((blocks, 2, per_core * NV, LANES), F32),
                pltpu.SemaphoreType.DMA,
                pltpu.SemaphoreType.DMA((2, blocks)),
                pltpu.SemaphoreType.DMA((2, blocks)),
                state,
                state,
                state,
                state,
                pltpu.VMEM((5 * CHANNELS, 3 * CHANNELS), BF16),
                pltpu.VMEM((2, per_core, LANES), jnp.int32),
                pltpu.VMEM((per_core, LANES), jnp.int32),
                pltpu.VMEM((2, CHANNELS, LANES), F32),
                pltpu.VMEM((2, blocks, CHANNELS, LANES), F32),
                pltpu.VMEM((2, CHANNELS, LANES), F32),
                pltpu.VMEM((2, 2, CHANNELS, LANES), F32),
                pltpu.SemaphoreType.DMA((3, per_core)),
                pltpu.SemaphoreType.DMA((3, per_core)),
                pltpu.SemaphoreType.DMA((3, per_core)),
                pltpu.SemaphoreType.DMA((2,)),
                pltpu.SemaphoreType.DMA((2, blocks)),
                pltpu.SemaphoreType.DMA((2, blocks)),
                pltpu.SemaphoreType.DMA((2, 2)),
                pltpu.SemaphoreType.DMA((2, 2)),
            ],
            compiler_params=pltpu.CompilerParams(
                collective_id=0, has_side_effects=True, vmem_limit_bytes=56 * 1024 * 1024
            ),
        )(start_state, source_term, time_step, wall_factor, flux_split.transpose(0, 2, 1, 3), stator, rotor)

    return jax.shard_map(
        local,
        mesh=mesh,
        in_specs=(
            P("ins", None, "grp", "blk"),
            P("ins", None, "grp", "blk"),
            P("grp", "blk"),
            P("grp", "blk"),
            P(),
            P("ins", "blk"),
            P("ins", "blk"),
        ),
        out_specs=P("ins", None, "grp", "blk"),
        check_vma=False,
    )
```

```python
import functools
import math

import jax
import jax.numpy as jnp
from jax import lax
from jax.experimental import pallas as pl
from jax.experimental.pallas import tpu as pltpu
from jax.sharding import PartitionSpec as P

NINST = 8
NV = 6
CHANNELS = NINST * NV
LANES = 128
PITCH_PAD = 8
GROUP = 16
CHUNKS = 4
SEGMENT_FACTORS = (1.0 / 3.0, 0.5, 1.0)
MESH = pl.DeviceIdType.MESH
F32 = jnp.float32
BF16 = jnp.bfloat16


def split_stack(values):
    high = values.astype(BF16)
    low = (values - high.astype(F32)).astype(BF16)
    return jnp.concatenate([high, low, high], axis=0)


def build_weights(flux_ref, weight_ref):
    shape = (NINST, 3 * CHANNELS)
    lane = lax.broadcasted_iota(jnp.int32, shape, 1)
    instance = lax.broadcasted_iota(jnp.int32, shape, 0)
    column = (
        lane
        - jnp.where(lane >= CHANNELS, CHANNELS, 0)
        - jnp.where(lane >= 2 * CHANNELS, CHANNELS, 0)
    )
    in_component = column >> 3
    offset = instance - (column & 7)
    spectral = jnp.zeros(shape, F32)
    for d in range(1, NINST):
        value = 0.5 * (-1.0) ** d * math.cos(math.pi * d / NINST) / math.sin(math.pi * d / NINST)
        spectral = jnp.where(offset == d, F32(value), spectral)
        spectral = jnp.where(offset == -d, F32(-value), spectral)
    same = offset == 0

    def flux_row(direction, part, v):
        row = jnp.zeros(shape, F32)
        for w in range(NV):
            row = jnp.where(in_component == w, flux_ref[direction, v, part, w], row)
        return row

    rows = [[], [], [], [], []]
    for v in range(NV):
        pa, ma = flux_row(0, 0, v), flux_row(0, 1, v)
        pc, mc = flux_row(1, 0, v), flux_row(1, 1, v)
        centre = jnp.where(same, pa - ma + pc - mc, 0.0) + jnp.where(
            in_component == v, spectral, 0.0
        )
        rows[0].append(centre)
        for place, matrix in ((1, ma), (2, -pa), (3, mc), (4, -pc)):
            rows[place].append(jnp.where(same, matrix, 0.0))
    flat = [row for group in rows for row in group]
    for k in range(0, len(flat), 2):
        value = jnp.concatenate([flat[k], flat[k + 1]], axis=0)
        high = value.astype(BF16).astype(F32)
        wide = lax.broadcasted_iota(jnp.int32, value.shape, 1)
        weight_ref[k * 8 : k * 8 + 16, :] = jnp.where(
            wide < 2 * CHANNELS, high, value - high
        ).astype(BF16)


def kernel(
    blocks,
    half,
    start_hbm,
    source_hbm,
    dt_hbm,
    wall_hbm,
    flux_ref,
    stator_hbm,
    rotor_hbm,
    out_hbm,
    dt_ref,
    wall_ref,
    stator_ref,
    rotor_ref,
    small_sem,
    out_sem,
    own,
    first_edge_send,
    first_edge_recv,
    first_edge_send_sem,
    first_edge_recv_sem,
    first_send,
    first_recv,
    first_sem,
    first_send_sem,
    first_recv_sem,
    state0,
    state1,
    state2,
    source,
    weight_ref,
    donors,
    donor_send,
    row_send,
    row_recv,
    edge_send,
    edge_recv,
    local_sem,
    remote_send_sem,
    remote_recv_sem,
    donor_sem,
    row_send_sem,
    row_recv_sem,
    edge_send_sem,
    edge_recv_sem,
):
    me = lax.axis_index("ins")
    blk = lax.axis_index("blk")
    other = 1 - me
    per_core = start_hbm.shape[0]
    pitch = half + PITCH_PAD
    right = lax.rem(blk + 1, blocks)
    left = lax.rem(blk + blocks - 1, blocks)
    my_rows = pl.ds(pl.multiple_of(me * half, 8), half)
    other_rows = pl.ds(pl.multiple_of(other * half, 8), half)

    def local_in(array, place, buffer, n):
        return pltpu.make_async_copy(
            array.at[n, :, my_rows, :],
            buffer.at[:, per_core * me + n, pl.ds(0, half), :],
            local_sem.at[place, n],
        )

    def remote_in(array, place, buffer, n):
        return pltpu.make_async_remote_copy(
            src_ref=array.at[n, :, other_rows, :],
            dst_ref=buffer.at[:, per_core * me + n, pl.ds(0, half), :],
            send_sem=remote_send_sem.at[place, n],
            recv_sem=remote_recv_sem.at[place, n],
            device_id={"ins": other},
            device_id_type=MESH,
        )

    first_copy = pltpu.make_async_copy(
        start_hbm, own.at[:, :, pl.ds(0, 2 * half), :], first_sem
    )
    first_copy.start()
    small = [
        pltpu.make_async_copy(stator_hbm, stator_ref, small_sem.at[0]),
        pltpu.make_async_copy(rotor_hbm, rotor_ref, small_sem.at[1]),
        pltpu.make_async_copy(dt_hbm.at[my_rows, :], dt_ref, small_sem.at[2]),
        pltpu.make_async_copy(wall_hbm.at[my_rows, :], wall_ref, small_sem.at[3]),
    ]
    for copy in small:
        copy.start()
    barrier = pltpu.get_barrier_semaphore()
    for b in range(blocks):
        pl.semaphore_signal(barrier, inc=1, device_id={"blk": b, "ins": other}, device_id_type=MESH)
    for d in range(1, blocks):
        pl.semaphore_signal(
            barrier, inc=1, device_id={"blk": lax.rem(blk + d, blocks)}, device_id_type=MESH
        )
    for n in range(per_core):
        local_in(start_hbm, 0, state0, n).start()
    for n in range(per_core):
        local_in(source_hbm, 1, source, n).start()
    build_weights(flux_ref, weight_ref)
    for copy in small:
        copy.wait()
    stator = stator_ref[...]
    rotor = rotor_ref[...]
    donors[me] = jnp.where(me == 0, stator, rotor)
    donor_send[...] = jnp.where(me == 0, rotor, stator)
    first_copy.wait()
    own_channels = per_core * NV
    own_pitch = 2 * half + PITCH_PAD
    flat_own = own.reshape(own_channels * own_pitch, LANES)

    def own_row(i):
        return flat_own[pl.ds(i, own_channels, stride=own_pitch), :]

    first_send[0] = own_row(half)
    first_send[1] = own_row(half - 1)
    first_recv[blk, me] = first_send[me]
    own_pair = lax.broadcasted_iota(jnp.int32, (own_channels, LANES), 1) >> 1

    def collect_own(t, edges):
        low, high = edges
        for k in range(8):
            i = t * 8 + k
            low = jnp.where(own_pair == i, pltpu.roll(own_row(i), 2 * i + 1, axis=1), low)
            high = jnp.where(
                own_pair == i, pltpu.roll(own_row(half + i), 2 * i + 1, axis=1), high
            )
        return low, high

    nothing = jnp.zeros((own_channels, LANES), F32)
    low_edges, high_edges = lax.fori_loop(0, half // 8, collect_own, (nothing, nothing))
    first_edge_send[0] = low_edges
    first_edge_send[1] = high_edges
    pl.semaphore_wait(barrier, 2 * blocks - 1)

    donor_copy = pltpu.make_async_remote_copy(
        src_ref=donor_send,
        dst_ref=donors.at[me],
        send_sem=donor_sem.at[0],
        recv_sem=donor_sem.at[1],
        device_id={"ins": other},
        device_id_type=MESH,
    )
    donor_copy.start()

    def first_edge_copy(core, side):
        return pltpu.make_async_remote_copy(
            src_ref=first_edge_send.at[core],
            dst_ref=first_edge_recv.at[side, me],
            send_sem=first_edge_send_sem.at[core, side],
            recv_sem=first_edge_recv_sem.at[side, me],
            device_id={"blk": right if side == 0 else left, "ins": core},
            device_id_type=MESH,
        )

    def first_edge_arrival(core, side):
        return pltpu.make_async_remote_copy(
            src_ref=first_edge_send.at[core],
            dst_ref=first_edge_recv.at[side, core],
            send_sem=first_edge_send_sem.at[core, side],
            recv_sem=first_edge_recv_sem.at[side, core],
            device_id={"blk": right if side == 0 else left, "ins": core},
            device_id_type=MESH,
        )

    first_edges = [(core, side) for core in range(2) for side in range(2)]

    def first_row_copy(core, b):
        return pltpu.make_async_remote_copy(
            src_ref=first_send.at[core],
            dst_ref=first_recv.at[blk, me],
            send_sem=first_send_sem.at[core, b],
            recv_sem=first_recv_sem.at[me, blk],
            device_id={"blk": b, "ins": core},
            device_id_type=MESH,
        )

    def first_row_arrival(core, b):
        return pltpu.make_async_remote_copy(
            src_ref=first_send.at[core],
            dst_ref=first_recv.at[b, core],
            send_sem=first_send_sem.at[core, b],
            recv_sem=first_recv_sem.at[core, b],
            device_id={"blk": b, "ins": core},
            device_id_type=MESH,
        )

    first_peers = [(me, lax.rem(blk + d, blocks)) for d in range(1, blocks)]
    first_peers += [(other, lax.rem(blk + d, blocks)) for d in range(blocks)]
    for core, b in first_peers:
        first_row_copy(core, b).start()
    for core, side in first_edges:
        first_edge_copy(core, side).start()
    for n in range(per_core):
        remote_in(start_hbm, 0, state0, n).start()
    for n in range(per_core):
        remote_in(source_hbm, 1, source, n).start()

    def row_copy(stage, b):
        return pltpu.make_async_remote_copy(
            src_ref=row_send.at[stage],
            dst_ref=row_recv.at[stage, blk],
            send_sem=row_send_sem.at[stage, b],
            recv_sem=row_recv_sem.at[stage, blk],
            device_id={"blk": b, "ins": other},
            device_id_type=MESH,
        )

    def row_arrival(stage, b):
        return pltpu.make_async_remote_copy(
            src_ref=row_send.at[stage],
            dst_ref=row_recv.at[stage, b],
            send_sem=row_send_sem.at[stage, b],
            recv_sem=row_recv_sem.at[stage, b],
            device_id={"blk": b, "ins": other},
            device_id_type=MESH,
        )

    def edge_copy(stage, side):
        return pltpu.make_async_remote_copy(
            src_ref=edge_send.at[stage],
            dst_ref=edge_recv.at[stage, side],
            send_sem=edge_send_sem.at[stage, side],
            recv_sem=edge_recv_sem.at[stage, side],
            device_id={"blk": right if side == 0 else left},
            device_id_type=MESH,
        )

    def send_row(stage):
        for b in range(blocks):
            row_copy(stage, b).start()

    def send_edges(stage):
        for side in range(2):
            edge_copy(stage, side).start()

    flat = {
        id(buffer): buffer.reshape(CHANNELS * pitch, LANES)
        for buffer in (state0, state1, state2, source)
    }

    def load_row(buffer, i):
        return flat[id(buffer)][pl.ds(i, CHANNELS, stride=pitch), :]

    def store_row(buffer, i, value):
        flat[id(buffer)][pl.ds(i, CHANNELS, stride=pitch), :] = value

    lane = lax.broadcasted_iota(jnp.int32, (CHANNELS, LANES), 1)
    first_lane = lane == 0
    last_lane = lane == LANES - 1
    edge_lane = first_lane | last_lane
    pair_index = lane >> 1
    even_lane = (lane & 1) == 0

    def step_row(i):
        return jnp.broadcast_to(dt_ref[pl.ds(i, 1), :], (CHANNELS, LANES))

    def wall_row(i):
        return jnp.broadcast_to(wall_ref[pl.ds(i, 1), :], (NINST, LANES))

    def main_pass(current, target, factor, halo, collect):
        def finish(i, total, edges):
            value = load_row(state0, i) - (factor * step_row(i)) * total
            store_row(target, i, value)
            if collect:
                edges = jnp.where(pair_index == i, pltpu.roll(value, 2 * i + 1, axis=1), edges)
            return edges

        def corrected(i):
            value = load_row(current, i)
            return value if halo is None else value - halo_at(halo, i)

        def group(t, carry):
            pending, behind, edges = carry
            first = t * GROUP
            for pair in range(GROUP // 2):
                rows = (first + 2 * pair, first + 2 * pair + 1)
                cells = [corrected(i) for i in rows]
                product = jnp.dot(
                    weight_ref[...],
                    split_stack(jnp.concatenate(cells, axis=1)),
                    preferred_element_type=F32,
                )
                for k in range(2):
                    i = rows[k]
                    centre, ahead, back, mc, pc = [
                        product[
                            CHANNELS * g : CHANNELS * (g + 1), LANES * k : LANES * (k + 1)
                        ]
                        for g in range(5)
                    ]
                    before = i - 1
                    if pair == 0 and k == 0:
                        before = jnp.maximum(before, 0)
                    edges = finish(before, pending + ahead, edges)
                    total = centre + behind - load_row(source, i)
                    total += jnp.where(last_lane, 0.0, pltpu.roll(mc, LANES - 1, axis=1))
                    total += jnp.where(first_lane, 0.0, pltpu.roll(pc, 1, axis=1))
                    turbulent = cells[k][CHANNELS - NINST :, :]
                    extra = 2.0 * turbulent * jnp.abs(turbulent) * wall_row(i)
                    pending = jnp.concatenate(
                        [total[: CHANNELS - NINST], total[CHANNELS - NINST :] + extra], axis=0
                    )
                    behind = back
            return pending, behind, edges

        zero = jnp.zeros((CHANNELS, LANES), F32)
        pending, _, edges = lax.fori_loop(0, half // GROUP, group, (zero, zero, zero))
        return finish(half - 1, pending, edges)

    interface_row = jnp.where(me == 0, half - 1, 0)

    def halo_products(stage):
        if stage == 0:
            for core, side in first_edges:
                first_edge_arrival(core, side).wait_recv()
            flat_edges = first_edge_recv.reshape(2 * CHANNELS, LANES)
            arrived = [
                jnp.concatenate(
                    [
                        flat_edges[pl.ds(side * CHANNELS + v, NINST, stride=NV), :]
                        for v in range(NV)
                    ],
                    axis=0,
                )
                for side in range(2)
            ]
        else:
            for side in range(2):
                edge_copy(stage - 1, side).wait_recv()
            arrived = [edge_recv[stage - 1, side] for side in range(2)]
        from_left = pltpu.roll(arrived[0], 1, axis=1)
        from_right = pltpu.roll(arrived[1], LANES - 1, axis=1)
        product = jnp.dot(
            weight_ref[3 * CHANNELS :, :],
            split_stack(jnp.concatenate([from_right, from_left], axis=1)),
            preferred_element_type=F32,
        )
        return jnp.where(even_lane, product[:CHANNELS, :LANES], product[CHANNELS:, LANES:])

    def halo_at(halo, i):
        return jnp.where(edge_lane, pltpu.roll(halo, LANES - 1 - 2 * i, axis=1), 0.0)

    def facing_product(stage):
        if stage == 0:
            for core, b in first_peers:
                first_row_arrival(core, b).wait_recv()
        flat_recv = first_recv.reshape(blocks * CHANNELS, LANES)

        def arrived(b, v):
            if stage == 0:
                return flat_recv[pl.ds(b * CHANNELS + v, NINST, stride=NV), :]
            return row_recv[stage - 1, b, v * NINST : (v + 1) * NINST, :]

        donor = jnp.concatenate([donors[0], donors[1]], axis=0)
        start = jnp.broadcast_to(donor[:, 0:1], (NINST, LANES))
        shift = start & (LANES - 1)
        block = start >> 7
        small_lane = lax.broadcasted_iota(jnp.int32, (NINST, LANES), 1)
        following = jnp.where(block == blocks - 1, 0, block + 1)
        wanted = jnp.where(small_lane >= shift, block, following)
        index = (small_lane + shift) & (LANES - 1)
        pieces = [jnp.zeros((NINST, LANES), F32)] * NV
        for b in range(blocks):
            if stage > 0:
                row_arrival(stage - 1, b).wait_recv()
            pieces = [jnp.where(wanted == b, arrived(b, v), pieces[v]) for v in range(NV)]
        pieces = [jnp.take_along_axis(piece, index, axis=1) for piece in pieces]
        facing = jnp.concatenate(pieces, axis=0)
        matrix = weight_ref[pl.ds(pl.multiple_of(CHANNELS * (1 + me), 16), CHANNELS), :]
        return jnp.dot(matrix, split_stack(facing), preferred_element_type=F32)

    def compact_steps(t, steps):
        for k in range(8):
            i = t * 8 + k
            row = jnp.broadcast_to(dt_ref[pl.ds(i, 1), :], (NINST, LANES))
            steps = jnp.where(small_pair == i, pltpu.roll(row, 2 * i + 1, axis=1), steps)
        return steps

    small_pair = lax.broadcasted_iota(jnp.int32, (NINST, LANES), 1) >> 1
    edge_steps = lax.fori_loop(0, half // 8, compact_steps, jnp.zeros((NINST, LANES), F32))
    edge_steps = jnp.concatenate([edge_steps] * NV, axis=0)

    final = state1
    chunk = half // CHUNKS

    def local_out(c, n):
        return pltpu.make_async_copy(
            final.at[:, per_core * me + n, pl.ds(c * chunk, chunk), :],
            out_hbm.at[n, :, pl.ds(pl.multiple_of(me * half + c * chunk, 8), chunk), :],
            out_sem.at[0, c, n],
        )

    def remote_out(c, n):
        return pltpu.make_async_remote_copy(
            src_ref=final.at[:, per_core * other + n, pl.ds(c * chunk, chunk), :],
            dst_ref=out_hbm.at[n, :, pl.ds(pl.multiple_of(me * half + c * chunk, 8), chunk), :],
            send_sem=out_sem.at[1, c, n],
            recv_sem=out_sem.at[2, c, n],
            device_id={"ins": other},
            device_id_type=MESH,
        )

    def last_pass(target, halo):
        for c in range(CHUNKS):

            def group(t, carry):
                for k in range(8):
                    i = c * chunk + t * 8 + k
                    store_row(target, i, load_row(target, i) - halo_at(halo, i))
                return carry

            lax.fori_loop(0, chunk // 8, group, 0)
            for n in range(per_core):
                remote_out(c, n).start()
            for n in range(per_core):
                local_out(c, n).start()

    for n in range(per_core):
        local_in(start_hbm, 0, state0, n).wait()
    for n in range(per_core):
        remote_in(start_hbm, 0, state0, n).wait_recv()
    donor_copy.wait_recv()
    for n in range(per_core):
        local_in(source_hbm, 1, source, n).wait()
    for n in range(per_core):
        remote_in(source_hbm, 1, source, n).wait_recv()

    buffers = (state0, state1, state2, state1)
    halo = None
    for stage, factor in enumerate(SEGMENT_FACTORS):
        target = buffers[stage + 1]
        edges = main_pass(buffers[stage], target, factor, halo, stage < 2)
        halo = (factor * edge_steps) * halo_products(stage)
        change = (factor * step_row(interface_row)) * facing_product(stage)
        value = load_row(target, interface_row) - change
        store_row(target, interface_row, value)
        if stage < 2:
            row_send[stage] = value - halo_at(halo, interface_row)
            send_row(stage)
            corner = pltpu.roll(change, 2 * interface_row + 1, axis=1)
            edge_send[stage] = (
                edges - halo - jnp.where(pair_index == interface_row, corner, 0.0)
            )
            send_edges(stage)
    last_pass(buffers[3], halo)

    donor_copy.wait_send()
    for n in range(per_core):
        remote_in(start_hbm, 0, state0, n).wait_send()
        remote_in(source_hbm, 1, source, n).wait_send()
    for core, b in first_peers:
        first_row_copy(core, b).wait_send()
    for core, side in first_edges:
        first_edge_copy(core, side).wait_send()
    for stage in range(2):
        for b in range(blocks):
            row_copy(stage, b).wait_send()
        for side in range(2):
            edge_copy(stage, side).wait_send()
    for c in range(CHUNKS):
        for n in range(per_core):
            local_out(c, n).wait()
            remote_out(c, n).wait()


def solution(mesh):
    blocks = mesh.shape["blk"]

    def local(start_state, source_term, time_step, wall_factor, flux_split, stator, rotor):
        per_core, _, rows, _ = start_state.shape
        half = rows // 2
        pitch = half + PITCH_PAD
        state = pltpu.VMEM((NV, NINST, pitch, LANES), F32)
        hbm = pl.BlockSpec(memory_space=pltpu.HBM)
        return pl.pallas_call(
            functools.partial(kernel, blocks, half),
            out_shape=pltpu.VMEM(start_state.shape, F32),
            in_specs=[
                hbm,
                hbm,
                hbm,
                hbm,
                pl.BlockSpec(memory_space=pltpu.SMEM),
                hbm,
                hbm,
            ],
            out_specs=pl.BlockSpec(memory_space=pl.ANY),
            scratch_shapes=[
                pltpu.VMEM((half, LANES), F32),
                pltpu.VMEM((half, LANES), F32),
                pltpu.VMEM((per_core, LANES), jnp.int32),
                pltpu.VMEM((per_core, LANES), jnp.int32),
                pltpu.SemaphoreType.DMA((4,)),
                pltpu.SemaphoreType.DMA((3, CHUNKS, per_core)),
                pltpu.VMEM((per_core, NV, rows + PITCH_PAD, LANES), F32),
                pltpu.VMEM((2, per_core * NV, LANES), F32),
                pltpu.VMEM((2, 2, per_core * NV, LANES), F32),
                pltpu.SemaphoreType.DMA((2, 2)),
                pltpu.SemaphoreType.DMA((2, 2)),
                pltpu.VMEM((2, per_core * NV, LANES), F32),
                pltpu.VMEM((blocks, 2, per_core * NV, LANES), F32),
                pltpu.SemaphoreType.DMA,
                pltpu.SemaphoreType.DMA((2, blocks)),
                pltpu.SemaphoreType.DMA((2, blocks)),
                state,
                state,
                state,
                state,
                pltpu.VMEM((5 * CHANNELS, 3 * CHANNELS), BF16),
                pltpu.VMEM((2, per_core, LANES), jnp.int32),
                pltpu.VMEM((per_core, LANES), jnp.int32),
                pltpu.VMEM((2, CHANNELS, LANES), F32),
                pltpu.VMEM((2, blocks, CHANNELS, LANES), F32),
                pltpu.VMEM((2, CHANNELS, LANES), F32),
                pltpu.VMEM((2, 2, CHANNELS, LANES), F32),
                pltpu.SemaphoreType.DMA((2, per_core)),
                pltpu.SemaphoreType.DMA((2, per_core)),
                pltpu.SemaphoreType.DMA((2, per_core)),
                pltpu.SemaphoreType.DMA((2,)),
                pltpu.SemaphoreType.DMA((2, blocks)),
                pltpu.SemaphoreType.DMA((2, blocks)),
                pltpu.SemaphoreType.DMA((2, 2)),
                pltpu.SemaphoreType.DMA((2, 2)),
            ],
            compiler_params=pltpu.CompilerParams(
                collective_id=0, has_side_effects=True, vmem_limit_bytes=56 * 1024 * 1024
            ),
        )(start_state, source_term, time_step, wall_factor, flux_split.transpose(0, 2, 1, 3), stator, rotor)

    return jax.shard_map(
        local,
        mesh=mesh,
        in_specs=(
            P("ins", None, "grp", "blk"),
            P("ins", None, "grp", "blk"),
            P("grp", "blk"),
            P("grp", "blk"),
            P(),
            P("ins", "blk"),
            P("ins", "blk"),
        ),
        out_specs=P("ins", None, "grp", "blk"),
        check_vma=False,
    )
```

```python
import functools
import math

import jax
import jax.numpy as jnp
from jax import lax
from jax.experimental import pallas as pl
from jax.experimental.pallas import tpu as pltpu
from jax.sharding import PartitionSpec as P

NINST = 8
NV = 6
CHANNELS = NINST * NV
LANES = 128
PITCH_PAD = 8
GROUP = 16
CHUNKS = 4
SEGMENT_FACTORS = (1.0 / 3.0, 0.5, 1.0)
MESH = pl.DeviceIdType.MESH
F32 = jnp.float32
BF16 = jnp.bfloat16


def split_stack(values):
    high = values.astype(BF16)
    low = (values - high.astype(F32)).astype(BF16)
    return jnp.concatenate([high, low, high], axis=0)


def build_weights(flux_ref, weight_ref):
    shape = (NINST, 3 * CHANNELS)
    lane = lax.broadcasted_iota(jnp.int32, shape, 1)
    instance = lax.broadcasted_iota(jnp.int32, shape, 0)
    column = (
        lane
        - jnp.where(lane >= CHANNELS, CHANNELS, 0)
        - jnp.where(lane >= 2 * CHANNELS, CHANNELS, 0)
    )
    in_component = column >> 3
    offset = instance - (column & 7)
    spectral = jnp.zeros(shape, F32)
    for d in range(1, NINST):
        value = 0.5 * (-1.0) ** d * math.cos(math.pi * d / NINST) / math.sin(math.pi * d / NINST)
        spectral = jnp.where(offset == d, F32(value), spectral)
        spectral = jnp.where(offset == -d, F32(-value), spectral)
    same = offset == 0

    def flux_row(direction, part, v):
        row = jnp.zeros(shape, F32)
        for w in range(NV):
            row = jnp.where(in_component == w, flux_ref[direction, v, part, w], row)
        return row

    rows = [[], [], [], [], []]
    for v in range(NV):
        pa, ma = flux_row(0, 0, v), flux_row(0, 1, v)
        pc, mc = flux_row(1, 0, v), flux_row(1, 1, v)
        centre = jnp.where(same, pa - ma + pc - mc, 0.0) + jnp.where(
            in_component == v, spectral, 0.0
        )
        rows[0].append(centre)
        for place, matrix in ((1, ma), (2, -pa), (3, mc), (4, -pc)):
            rows[place].append(jnp.where(same, matrix, 0.0))
    flat = [row for group in rows for row in group]
    for k in range(0, len(flat), 2):
        value = jnp.concatenate([flat[k], flat[k + 1]], axis=0)
        high = value.astype(BF16).astype(F32)
        wide = lax.broadcasted_iota(jnp.int32, value.shape, 1)
        weight_ref[k * 8 : k * 8 + 16, :] = jnp.where(
            wide < 2 * CHANNELS, high, value - high
        ).astype(BF16)


def kernel(
    blocks,
    half,
    start_hbm,
    source_hbm,
    dt_hbm,
    wall_hbm,
    flux_ref,
    stator_hbm,
    rotor_hbm,
    out_hbm,
    dt_ref,
    wall_ref,
    stator_ref,
    rotor_ref,
    small_sem,
    out_sem,
    own,
    first_edge_send,
    first_edge_recv,
    first_edge_send_sem,
    first_edge_recv_sem,
    first_send,
    first_recv,
    first_sem,
    first_send_sem,
    first_recv_sem,
    state0,
    state1,
    state2,
    source,
    weight_ref,
    donors,
    donor_send,
    row_send,
    row_recv,
    edge_send,
    edge_recv,
    local_sem,
    remote_send_sem,
    remote_recv_sem,
    donor_sem,
    row_send_sem,
    row_recv_sem,
    edge_send_sem,
    edge_recv_sem,
):
    me = lax.axis_index("ins")
    blk = lax.axis_index("blk")
    other = 1 - me
    per_core = start_hbm.shape[0]
    pitch = half + PITCH_PAD
    right = lax.rem(blk + 1, blocks)
    left = lax.rem(blk + blocks - 1, blocks)
    my_rows = pl.ds(pl.multiple_of(me * half, 8), half)
    other_rows = pl.ds(pl.multiple_of(other * half, 8), half)

    def local_in(array, place, buffer, n):
        return pltpu.make_async_copy(
            array.at[n, :, my_rows, :],
            buffer.at[:, per_core * me + n, pl.ds(0, half), :],
            local_sem.at[place, n],
        )

    def remote_in(array, place, buffer, n):
        return pltpu.make_async_remote_copy(
            src_ref=array.at[n, :, other_rows, :],
            dst_ref=buffer.at[:, per_core * me + n, pl.ds(0, half), :],
            send_sem=remote_send_sem.at[place, n],
            recv_sem=remote_recv_sem.at[place, n],
            device_id={"ins": other},
            device_id_type=MESH,
        )

    first_copy = pltpu.make_async_copy(
        start_hbm, own.at[:, :, pl.ds(0, 2 * half), :], first_sem
    )
    first_copy.start()
    small = [
        pltpu.make_async_copy(stator_hbm, stator_ref, small_sem.at[0]),
        pltpu.make_async_copy(rotor_hbm, rotor_ref, small_sem.at[1]),
        pltpu.make_async_copy(dt_hbm.at[my_rows, :], dt_ref, small_sem.at[2]),
        pltpu.make_async_copy(wall_hbm.at[my_rows, :], wall_ref, small_sem.at[3]),
    ]
    for copy in small:
        copy.start()
    barrier = pltpu.get_barrier_semaphore()
    for b in range(blocks):
        pl.semaphore_signal(barrier, inc=1, device_id={"blk": b, "ins": other}, device_id_type=MESH)
    for d in range(1, blocks):
        pl.semaphore_signal(
            barrier, inc=1, device_id={"blk": lax.rem(blk + d, blocks)}, device_id_type=MESH
        )
    for n in range(per_core):
        local_in(start_hbm, 0, state0, n).start()
    for n in range(per_core):
        local_in(source_hbm, 1, source, n).start()
    build_weights(flux_ref, weight_ref)
    for copy in small:
        copy.wait()
    stator = stator_ref[...]
    rotor = rotor_ref[...]
    donors[me] = jnp.where(me == 0, stator, rotor)
    donor_send[...] = jnp.where(me == 0, rotor, stator)
    first_copy.wait()
    own_channels = per_core * NV
    own_pitch = 2 * half + PITCH_PAD
    flat_own = own.reshape(own_channels * own_pitch, LANES)

    def own_row(i):
        return flat_own[pl.ds(i, own_channels, stride=own_pitch), :]

    first_send[0] = own_row(half)
    first_send[1] = own_row(half - 1)
    first_recv[blk, me] = first_send[me]
    own_pair = lax.broadcasted_iota(jnp.int32, (own_channels, LANES), 1) >> 1

    def collect_own(t, edges):
        low, high = edges
        for k in range(8):
            i = t * 8 + k
            low = jnp.where(own_pair == i, pltpu.roll(own_row(i), 2 * i + 1, axis=1), low)
            high = jnp.where(
                own_pair == i, pltpu.roll(own_row(half + i), 2 * i + 1, axis=1), high
            )
        return low, high

    nothing = jnp.zeros((own_channels, LANES), F32)
    low_edges, high_edges = lax.fori_loop(0, half // 8, collect_own, (nothing, nothing))
    first_edge_send[0] = low_edges
    first_edge_send[1] = high_edges
    pl.semaphore_wait(barrier, 2 * blocks - 1)

    donor_copy = pltpu.make_async_remote_copy(
        src_ref=donor_send,
        dst_ref=donors.at[me],
        send_sem=donor_sem.at[0],
        recv_sem=donor_sem.at[1],
        device_id={"ins": other},
        device_id_type=MESH,
    )
    donor_copy.start()

    def first_edge_copy(core, side):
        return pltpu.make_async_remote_copy(
            src_ref=first_edge_send.at[core],
            dst_ref=first_edge_recv.at[side, me],
            send_sem=first_edge_send_sem.at[core, side],
            recv_sem=first_edge_recv_sem.at[side, me],
            device_id={"blk": right if side == 0 else left, "ins": core},
            device_id_type=MESH,
        )

    def first_edge_arrival(core, side):
        return pltpu.make_async_remote_copy(
            src_ref=first_edge_send.at[core],
            dst_ref=first_edge_recv.at[side, core],
            send_sem=first_edge_send_sem.at[core, side],
            recv_sem=first_edge_recv_sem.at[side, core],
            device_id={"blk": right if side == 0 else left, "ins": core},
            device_id_type=MESH,
        )

    first_edges = [(core, side) for core in range(2) for side in range(2)]

    def first_row_copy(core, b):
        return pltpu.make_async_remote_copy(
            src_ref=first_send.at[core],
            dst_ref=first_recv.at[blk, me],
            send_sem=first_send_sem.at[core, b],
            recv_sem=first_recv_sem.at[me, blk],
            device_id={"blk": b, "ins": core},
            device_id_type=MESH,
        )

    def first_row_arrival(core, b):
        return pltpu.make_async_remote_copy(
            src_ref=first_send.at[core],
            dst_ref=first_recv.at[b, core],
            send_sem=first_send_sem.at[core, b],
            recv_sem=first_recv_sem.at[core, b],
            device_id={"blk": b, "ins": core},
            device_id_type=MESH,
        )

    first_peers = [(me, lax.rem(blk + d, blocks)) for d in range(1, blocks)]
    first_peers += [(other, lax.rem(blk + d, blocks)) for d in range(blocks)]
    for core, b in first_peers:
        first_row_copy(core, b).start()
    for core, side in first_edges:
        first_edge_copy(core, side).start()
    for n in range(per_core):
        remote_in(start_hbm, 0, state0, n).start()
    for n in range(per_core):
        remote_in(source_hbm, 1, source, n).start()

    def row_copy(stage, b):
        return pltpu.make_async_remote_copy(
            src_ref=row_send.at[stage],
            dst_ref=row_recv.at[stage, blk],
            send_sem=row_send_sem.at[stage, b],
            recv_sem=row_recv_sem.at[stage, blk],
            device_id={"blk": b, "ins": other},
            device_id_type=MESH,
        )

    def row_arrival(stage, b):
        return pltpu.make_async_remote_copy(
            src_ref=row_send.at[stage],
            dst_ref=row_recv.at[stage, b],
            send_sem=row_send_sem.at[stage, b],
            recv_sem=row_recv_sem.at[stage, b],
            device_id={"blk": b, "ins": other},
            device_id_type=MESH,
        )

    def edge_copy(stage, side):
        return pltpu.make_async_remote_copy(
            src_ref=edge_send.at[stage],
            dst_ref=edge_recv.at[stage, side],
            send_sem=edge_send_sem.at[stage, side],
            recv_sem=edge_recv_sem.at[stage, side],
            device_id={"blk": right if side == 0 else left},
            device_id_type=MESH,
        )

    def send_row(stage):
        for b in range(blocks):
            row_copy(stage, b).start()

    def send_edges(stage):
        for side in range(2):
            edge_copy(stage, side).start()

    flat = {
        id(buffer): buffer.reshape(CHANNELS * pitch, LANES)
        for buffer in (state0, state1, state2, source)
    }

    def load_row(buffer, i):
        return flat[id(buffer)][pl.ds(i, CHANNELS, stride=pitch), :]

    def store_row(buffer, i, value):
        flat[id(buffer)][pl.ds(i, CHANNELS, stride=pitch), :] = value

    lane = lax.broadcasted_iota(jnp.int32, (CHANNELS, LANES), 1)
    first_lane = lane == 0
    last_lane = lane == LANES - 1
    edge_lane = first_lane | last_lane
    pair_index = lane >> 1
    even_lane = (lane & 1) == 0

    def step_row(i):
        return jnp.broadcast_to(dt_ref[pl.ds(i, 1), :], (CHANNELS, LANES))

    def wall_row(i):
        return jnp.broadcast_to(wall_ref[pl.ds(i, 1), :], (NINST, LANES))

    def main_pass(current, target, factor, halo, collect):
        def finish(i, total, edges):
            value = load_row(state0, i) - (factor * step_row(i)) * total
            store_row(target, i, value)
            if collect:
                edges = jnp.where(pair_index == i, pltpu.roll(value, 2 * i + 1, axis=1), edges)
            return edges

        def corrected(i):
            value = load_row(current, i)
            return value if halo is None else value - halo_at(halo, i)

        def group(t, carry):
            pending, behind, edges = carry
            first = t * GROUP
            for pair in range(GROUP // 2):
                rows = (first + 2 * pair, first + 2 * pair + 1)
                cells = [corrected(i) for i in rows]
                product = jnp.dot(
                    weight_ref[...],
                    split_stack(jnp.concatenate(cells, axis=1)),
                    preferred_element_type=F32,
                )
                for k in range(2):
                    i = rows[k]
                    centre, ahead, back, mc, pc = [
                        product[
                            CHANNELS * g : CHANNELS * (g + 1), LANES * k : LANES * (k + 1)
                        ]
                        for g in range(5)
                    ]
                    before = i - 1
                    if pair == 0 and k == 0:
                        before = jnp.maximum(before, 0)
                    edges = finish(before, pending + ahead, edges)
                    total = centre + behind - load_row(source, i)
                    total += jnp.where(last_lane, 0.0, pltpu.roll(mc, LANES - 1, axis=1))
                    total += jnp.where(first_lane, 0.0, pltpu.roll(pc, 1, axis=1))
                    turbulent = cells[k][CHANNELS - NINST :, :]
                    extra = 2.0 * turbulent * jnp.abs(turbulent) * wall_row(i)
                    pending = jnp.concatenate(
                        [total[: CHANNELS - NINST], total[CHANNELS - NINST :] + extra], axis=0
                    )
                    behind = back
            return pending, behind, edges

        zero = jnp.zeros((CHANNELS, LANES), F32)
        pending, _, edges = lax.fori_loop(0, half // GROUP, group, (zero, zero, zero))
        return finish(half - 1, pending, edges)

    interface_row = jnp.where(me == 0, half - 1, 0)

    def halo_products(stage):
        if stage == 0:
            for core, side in first_edges:
                first_edge_arrival(core, side).wait_recv()
            flat_edges = first_edge_recv.reshape(2 * CHANNELS, LANES)
            arrived = [
                jnp.concatenate(
                    [
                        flat_edges[pl.ds(side * CHANNELS + v, NINST, stride=NV), :]
                        for v in range(NV)
                    ],
                    axis=0,
                )
                for side in range(2)
            ]
        else:
            for side in range(2):
                edge_copy(stage - 1, side).wait_recv()
            arrived = [edge_recv[stage - 1, side] for side in range(2)]
        from_left = pltpu.roll(arrived[0], 1, axis=1)
        from_right = pltpu.roll(arrived[1], LANES - 1, axis=1)
        product = jnp.dot(
            weight_ref[3 * CHANNELS :, :],
            split_stack(jnp.concatenate([from_right, from_left], axis=1)),
            preferred_element_type=F32,
        )
        return jnp.where(even_lane, product[:CHANNELS, :LANES], product[CHANNELS:, LANES:])

    def halo_at(halo, i):
        return jnp.where(edge_lane, pltpu.roll(halo, LANES - 1 - 2 * i, axis=1), 0.0)

    def facing_product(stage):
        if stage == 0:
            for core, b in first_peers:
                first_row_arrival(core, b).wait_recv()
        flat_recv = first_recv.reshape(blocks * CHANNELS, LANES)

        def arrived(b, v):
            if stage == 0:
                return flat_recv[pl.ds(b * CHANNELS + v, NINST, stride=NV), :]
            return row_recv[stage - 1, b, v * NINST : (v + 1) * NINST, :]

        donor = jnp.concatenate([donors[0], donors[1]], axis=0)
        start = jnp.broadcast_to(donor[:, 0:1], (NINST, LANES))
        shift = start & (LANES - 1)
        block = start >> 7
        small_lane = lax.broadcasted_iota(jnp.int32, (NINST, LANES), 1)
        following = jnp.where(block == blocks - 1, 0, block + 1)
        wanted = jnp.where(small_lane >= shift, block, following)
        index = (small_lane + shift) & (LANES - 1)
        pieces = [jnp.zeros((NINST, LANES), F32)] * NV
        for b in range(blocks):
            if stage > 0:
                row_arrival(stage - 1, b).wait_recv()
            pieces = [jnp.where(wanted == b, arrived(b, v), pieces[v]) for v in range(NV)]
        pieces = [jnp.take_along_axis(piece, index, axis=1) for piece in pieces]
        facing = jnp.concatenate(pieces, axis=0)
        matrix = weight_ref[pl.ds(pl.multiple_of(CHANNELS * (1 + me), 16), CHANNELS), :]
        return jnp.dot(matrix, split_stack(facing), preferred_element_type=F32)

    def compact_steps(t, steps):
        for k in range(8):
            i = t * 8 + k
            row = jnp.broadcast_to(dt_ref[pl.ds(i, 1), :], (NINST, LANES))
            steps = jnp.where(small_pair == i, pltpu.roll(row, 2 * i + 1, axis=1), steps)
        return steps

    small_pair = lax.broadcasted_iota(jnp.int32, (NINST, LANES), 1) >> 1
    edge_steps = lax.fori_loop(0, half // 8, compact_steps, jnp.zeros((NINST, LANES), F32))
    edge_steps = jnp.concatenate([edge_steps] * NV, axis=0)

    final = state1
    chunk = half // CHUNKS

    def local_out(c, n):
        return pltpu.make_async_copy(
            final.at[:, per_core * me + n, pl.ds(c * chunk, chunk), :],
            out_hbm.at[n, :, pl.ds(pl.multiple_of(me * half + c * chunk, 8), chunk), :],
            out_sem.at[0, c, n],
        )

    def remote_out(c, n):
        return pltpu.make_async_remote_copy(
            src_ref=final.at[:, per_core * other + n, pl.ds(c * chunk, chunk), :],
            dst_ref=out_hbm.at[n, :, pl.ds(pl.multiple_of(me * half + c * chunk, 8), chunk), :],
            send_sem=out_sem.at[1, c, n],
            recv_sem=out_sem.at[2, c, n],
            device_id={"ins": other},
            device_id_type=MESH,
        )

    def last_pass(target, halo):
        for c in range(CHUNKS):

            def group(t, carry):
                for k in range(8):
                    i = c * chunk + t * 8 + k
                    store_row(target, i, load_row(target, i) - halo_at(halo, i))
                return carry

            lax.fori_loop(0, chunk // 8, group, 0)
            for n in range(per_core):
                remote_out(c, n).start()
            for n in range(per_core):
                local_out(c, n).start()

    for n in range(per_core):
        local_in(start_hbm, 0, state0, n).wait()
    for n in range(per_core):
        remote_in(start_hbm, 0, state0, n).wait_recv()
    donor_copy.wait_recv()
    for n in range(per_core):
        local_in(source_hbm, 1, source, n).wait()
    for n in range(per_core):
        remote_in(source_hbm, 1, source, n).wait_recv()

    buffers = (state0, state1, state2, state1)
    halo = None
    for stage, factor in enumerate(SEGMENT_FACTORS):
        target = buffers[stage + 1]
        edges = main_pass(buffers[stage], target, factor, halo, stage < 2)
        halo = (factor * edge_steps) * halo_products(stage)
        change = (factor * step_row(interface_row)) * facing_product(stage)
        value = load_row(target, interface_row) - change
        store_row(target, interface_row, value)
        if stage < 2:
            row_send[stage] = value - halo_at(halo, interface_row)
            corner = pltpu.roll(change, 2 * interface_row + 1, axis=1)
            edge_send[stage] = (
                edges - halo - jnp.where(pair_index == interface_row, corner, 0.0)
            )
            send_edges(stage)
            send_row(stage)
    last_pass(buffers[3], halo)

    donor_copy.wait_send()
    for n in range(per_core):
        remote_in(start_hbm, 0, state0, n).wait_send()
        remote_in(source_hbm, 1, source, n).wait_send()
    for core, b in first_peers:
        first_row_copy(core, b).wait_send()
    for core, side in first_edges:
        first_edge_copy(core, side).wait_send()
    for stage in range(2):
        for b in range(blocks):
            row_copy(stage, b).wait_send()
        for side in range(2):
            edge_copy(stage, side).wait_send()
    for c in range(CHUNKS):
        for n in range(per_core):
            local_out(c, n).wait()
            remote_out(c, n).wait()


def solution(mesh):
    blocks = mesh.shape["blk"]

    def local(start_state, source_term, time_step, wall_factor, flux_split, stator, rotor):
        per_core, _, rows, _ = start_state.shape
        half = rows // 2
        pitch = half + PITCH_PAD
        state = pltpu.VMEM((NV, NINST, pitch, LANES), F32)
        hbm = pl.BlockSpec(memory_space=pltpu.HBM)
        return pl.pallas_call(
            functools.partial(kernel, blocks, half),
            out_shape=pltpu.VMEM(start_state.shape, F32),
            in_specs=[
                hbm,
                hbm,
                hbm,
                hbm,
                pl.BlockSpec(memory_space=pltpu.SMEM),
                hbm,
                hbm,
            ],
            out_specs=pl.BlockSpec(memory_space=pl.ANY),
            scratch_shapes=[
                pltpu.VMEM((half, LANES), F32),
                pltpu.VMEM((half, LANES), F32),
                pltpu.VMEM((per_core, LANES), jnp.int32),
                pltpu.VMEM((per_core, LANES), jnp.int32),
                pltpu.SemaphoreType.DMA((4,)),
                pltpu.SemaphoreType.DMA((3, CHUNKS, per_core)),
                pltpu.VMEM((per_core, NV, rows + PITCH_PAD, LANES), F32),
                pltpu.VMEM((2, per_core * NV, LANES), F32),
                pltpu.VMEM((2, 2, per_core * NV, LANES), F32),
                pltpu.SemaphoreType.DMA((2, 2)),
                pltpu.SemaphoreType.DMA((2, 2)),
                pltpu.VMEM((2, per_core * NV, LANES), F32),
                pltpu.VMEM((blocks, 2, per_core * NV, LANES), F32),
                pltpu.SemaphoreType.DMA,
                pltpu.SemaphoreType.DMA((2, blocks)),
                pltpu.SemaphoreType.DMA((2, blocks)),
                state,
                state,
                state,
                state,
                pltpu.VMEM((5 * CHANNELS, 3 * CHANNELS), BF16),
                pltpu.VMEM((2, per_core, LANES), jnp.int32),
                pltpu.VMEM((per_core, LANES), jnp.int32),
                pltpu.VMEM((2, CHANNELS, LANES), F32),
                pltpu.VMEM((2, blocks, CHANNELS, LANES), F32),
                pltpu.VMEM((2, CHANNELS, LANES), F32),
                pltpu.VMEM((2, 2, CHANNELS, LANES), F32),
                pltpu.SemaphoreType.DMA((2, per_core)),
                pltpu.SemaphoreType.DMA((2, per_core)),
                pltpu.SemaphoreType.DMA((2, per_core)),
                pltpu.SemaphoreType.DMA((2,)),
                pltpu.SemaphoreType.DMA((2, blocks)),
                pltpu.SemaphoreType.DMA((2, blocks)),
                pltpu.SemaphoreType.DMA((2, 2)),
                pltpu.SemaphoreType.DMA((2, 2)),
            ],
            compiler_params=pltpu.CompilerParams(
                collective_id=0, has_side_effects=True, vmem_limit_bytes=56 * 1024 * 1024
            ),
        )(start_state, source_term, time_step, wall_factor, flux_split.transpose(0, 2, 1, 3), stator, rotor)

    return jax.shard_map(
        local,
        mesh=mesh,
        in_specs=(
            P("ins", None, "grp", "blk"),
            P("ins", None, "grp", "blk"),
            P("grp", "blk"),
            P("grp", "blk"),
            P(),
            P("ins", "blk"),
            P("ins", "blk"),
        ),
        out_specs=P("ins", None, "grp", "blk"),
        check_vma=False,
    )
```
